32 devices in a mesh: ctx: 8 (over z, core), adp: 4 (over y, x).
Axes of the slice: x: 2, y: 2, z: 4, core: 2. Of those that a mesh axis runs over, the one named last changes fastest.
Arguments:
- queries: bfloat16 [2048, 4096], P('ctx', 'adp'), may hold values from -100 to 100
- keys: bfloat16 [2048, 512], P('ctx'), may hold values from -5 to 5
- values: bfloat16 [2048, 512], P('ctx'), may hold values from -6 to 6
- grad_out: bfloat16 [2048, 4096], P('ctx', 'adp'), may hold values from -6 to 6
- docs: int32 [2048], P('ctx'), may hold values from 0 to 15, never falling along the last dimension, each value on 1 to 1536 neighbouring positions
- block_tenant: int32 [16], P('ctx'), may hold values from 0 to 3
- low_rank: bfloat16 [2048, 64], P('ctx'), may hold values from -6 to 6
- adapter_b: bfloat16 [4, 64, 4096], P('adp'), may hold values from -0.75 to 0.75
Outputs:
- grad_queries: bfloat16 [2048, 4096], P('ctx', 'adp')
- grad_low_rank: float32 [2048, 64], P(('ctx', 'adp'))
- grad_adapter: float32 [4, 64, 4096], P('adp', None, 'ctx')
The draws below stay inside these ranges and needn't reach their ends.
Inputs may be any that keep to these rules, and one draw needn't show every extreme that they name: docs never falls from one position to the next.
All inputs are finite; a program needn't handle non-finite values.
Results may differ from the reference program's by a relative error of at most 0.019.
Values may be sent and summed in bfloat16 or wider, within the bound.
No kernel may reach another device: no remote copies, remote signals or barrier semaphores. Data moves between devices by JAX's collectives and lax.ppermute only.
A program may use at most 64 MiB of HBM per device.

```python
import math
import jax
import jax.numpy as jnp
import numpy as np
from jax import lax

QH = 32
KVH = 4
HD = 128
RANK = 64
BLOCK = 128
TOK_DEV = 256
LENGTH = 2048
TENANTS = 4
N_CTX = 8


def aligned_parts(key):
    base = jax.random.normal(jax.random.fold_in(key, 101), (LENGTH, KVH * HD), jnp.float32)
    base = jnp.clip(base, -5.0, 5.0)
    base = base.at[0, 0].set(5.0)
    base = base.at[2, 0].set(-5.0)
    return base


def draw_keys(key, part):
    base = aligned_parts(key)
    return base.astype(jnp.bfloat16)


def draw_queries(key, part):
    fresh = jax.random.normal(jax.random.fold_in(key, 104), (LENGTH, QH * HD), jnp.float32)
    fresh = jnp.clip(fresh, -6.0, 6.0)
    return fresh.astype(jnp.bfloat16)


def set_ends(entries, own_key, least, top_value):
    dims = entries.shape
    index_at = [jax.random.randint(jax.random.fold_in(own_key, axis), (), 0, dims[axis]) for axis in range(len(dims))]
    entries = entries.at[tuple(index_at)].set(least)
    longest = dims.index(max(dims))
    index_at[longest] = (index_at[longest] + 1) % dims[longest]
    return entries.at[tuple(index_at)].set(top_value)


def block_scale(own_key, shape, pieces, least, high):
    def one(position, shards_of):
        steps = jax.random.uniform(jax.random.fold_in(jax.random.fold_in(own_key, 6), position), (shards_of,), jnp.float32, least / len(pieces), high / len(pieces))
        return jnp.repeat(jnp.exp(steps), shape[position] // shards_of).reshape((-1,) + (1,) * (len(shape) - position - 1))

    loudness = one(*pieces[0])
    for cut in pieces[1:]:
        loudness = loudness * one(*cut)
    return loudness


def rank_bounds(amount, slope):
    portions = [(1 << 20) // math.isqrt(rank ** slope) + 1 for rank in range(1, amount + 1)]
    scale = 1 + sum(portions) // (1 << 30)
    return np.cumsum(np.array([max(1, weight // scale) for weight in portions]))


def ranked(key, extent, count, lean):
    listing = rank_bounds(count, lean)
    ticket = jax.random.randint(jax.random.fold_in(key, 1), extent, 0, int(listing[count - 1]))
    standing = jnp.searchsorted(jnp.asarray(listing, jnp.int32), ticket, side="right")
    return jax.random.permutation(jax.random.fold_in(key, 2), count)[standing].astype(jnp.int32)


def split_up(count, total, limit, slope):
    loads = [(1 << 20) // math.isqrt(grade ** slope) + 1 for grade in range(2, count + 1)]
    rest, counts = total - limit - (count - 1), [1] * (count - 1)
    while rest > 0:
        movable = [i for i in range(count - 1) if counts[i] < limit]
        pool, budget = sum([loads[i] for i in movable]), rest
        for i in movable:
            addition = min(limit - counts[i], max(1, budget * loads[i] // pool), rest)
            counts[i] = counts[i] + addition
            rest = rest - addition
    return np.array([limit] + counts)


def uneven_parts(rng, number_of, total, most, slope):
    if number_of == 2:
        one = jax.random.randint(rng, (), max(1, total - most), min(most, total - 1) + 1)
        return jnp.stack([one, total - one])
    tallies = jnp.asarray(split_up(number_of, total, most, slope), jnp.int32)
    couples = (number_of - 1) // 2
    giver, taker = tallies[1:1 + 2 * couples:2], tallies[2:2 + 2 * couples:2]
    slack = jnp.minimum(giver - 1, most - taker)
    passed = jax.random.randint(jax.random.fold_in(rng, 1), (couples,), 0, 1 << 20) % (slack + 1)
    tallies = tallies.at[1:1 + 2 * couples:2].set(giver - passed).at[2:2 + 2 * couples:2].set(taker + passed)
    return tallies[jax.random.permutation(jax.random.fold_in(rng, 2), number_of)]


def bell_draw(stream_key, dims, scale, bound, cuts=(), kind=jnp.bfloat16):
    array = scale * jax.random.normal(stream_key, dims, jnp.float32)
    if cuts:
        array = array * block_scale(stream_key, dims, cuts, -0.22, 0.18)
    return jnp.clip(array, -bound, bound).astype(kind)


def setup_inputs(seed: int = 0) -> dict:
    streams_of = jax.random.split(jax.random.key(seed), 9)
    return {
        "queries": draw_queries(jax.random.fold_in(streams_of[8], 71), 0),
        "keys": draw_keys(jax.random.fold_in(streams_of[8], 71), 0),
        "values": bell_draw(streams_of[2], (LENGTH, KVH * HD), 1.0, 6.0, ((0, 8),)),
        "grad_out": bell_draw(streams_of[3], (LENGTH, QH * HD), 1.0, 6.0, ((0, 8), (1, 4))),
        "docs": jnp.searchsorted(jnp.cumsum(uneven_parts(streams_of[4], 2 * N_CTX, LENGTH, 3 * LENGTH // 4, 0)), jnp.arange(LENGTH), side="right").astype(jnp.int32),
        "block_tenant": set_ends(ranked(streams_of[5], (LENGTH // BLOCK,), TENANTS, 2), jax.random.fold_in(streams_of[5], 3), 0, TENANTS - 1).astype(jnp.int32),
        "low_rank": bell_draw(streams_of[6], (LENGTH, RANK), 1.0, 6.0, ((0, 8),)),
        "adapter_b": bell_draw(streams_of[7], (TENANTS, RANK, QH * HD), RANK ** -0.5, 0.75, ((0, 4),)),
    }


def head_grads(query_head, key_head, value_head, grad_head, docs, positions):
    logit_scale = HD ** -0.5

    def one_block(block_index):
        row_start = (block_index * TOK_DEV).astype(jnp.int32)
        query_block = lax.dynamic_slice_in_dim(query_head, row_start, TOK_DEV, 0)
        grad_block = lax.dynamic_slice_in_dim(grad_head, row_start, TOK_DEV, 0)
        query_pos = lax.dynamic_slice_in_dim(positions, row_start, TOK_DEV, 0)
        query_doc = lax.dynamic_slice_in_dim(docs, row_start, TOK_DEV, 0)
        scores = jnp.dot(query_block, key_head.T, preferred_element_type=jnp.float32) * logit_scale
        visible = (positions[None, :] <= query_pos[:, None]) & (docs[None, :] == query_doc[:, None])
        row_top = jnp.max(jnp.where(visible, scores, -1e30), axis=1)
        row_total = jnp.sum(jnp.where(visible, jnp.exp(scores - row_top[:, None]), 0.0), axis=1)
        log_total = row_top + jnp.log(row_total)
        weights = jnp.where(visible, jnp.exp(scores - log_total[:, None]), 0.0)
        attended = jnp.dot(weights.astype(jnp.bfloat16), value_head, preferred_element_type=jnp.float32)
        row_delta = jnp.sum(grad_block.astype(jnp.float32) * attended, axis=1)
        grad_weights = jnp.dot(grad_block, value_head.T, preferred_element_type=jnp.float32)
        grad_scores = (weights * (grad_weights - row_delta[:, None])).astype(jnp.bfloat16)
        result = jnp.dot(grad_scores, key_head, preferred_element_type=jnp.float32) * logit_scale
        return result.astype(jnp.bfloat16)

    blocks = lax.map(one_block, jnp.arange(LENGTH // TOK_DEV, dtype=jnp.int32))
    return blocks.reshape(LENGTH, HD)


def reference(queries, keys, values, grad_out, docs, block_tenant, low_rank, adapter_b):
    group = QH // KVH
    positions = jnp.arange(LENGTH, dtype=jnp.int32)
    query_heads = queries.reshape(LENGTH, QH, HD).transpose(1, 0, 2)
    grad_heads = grad_out.reshape(LENGTH, QH, HD).transpose(1, 0, 2)
    key_heads = keys.reshape(LENGTH, KVH, HD).transpose(1, 0, 2)
    value_heads = values.reshape(LENGTH, KVH, HD).transpose(1, 0, 2)

    def per_head(head_index):
        kv_index = head_index // group
        return head_grads(query_heads[head_index], key_heads[kv_index], value_heads[kv_index], grad_heads[head_index], docs, positions)

    grads = lax.map(per_head, jnp.arange(QH, dtype=jnp.int32))
    grad_queries = grads.transpose(1, 0, 2).reshape(LENGTH, QH * HD)

    block_count = LENGTH // BLOCK
    grad_blocks = grad_queries.reshape(block_count, BLOCK, QH * HD)
    low_blocks = low_rank.reshape(block_count, BLOCK, RANK)

    def block_step(adapter_acc, inputs):
        grad_block, low_block, tenant = inputs
        chosen = adapter_b[tenant]
        rank_block = jnp.dot(grad_block, chosen.T, preferred_element_type=jnp.float32) * 2.0
        term = jnp.dot(low_block.T, grad_block, preferred_element_type=jnp.float32) * 2.0
        adapter_acc = adapter_acc.at[tenant].add(term)
        return adapter_acc, rank_block

    start_acc = jnp.zeros((TENANTS, RANK, QH * HD), jnp.float32)
    grad_adapter, rank_blocks = lax.scan(block_step, start_acc, (grad_blocks, low_blocks, block_tenant))
    grad_low_rank = rank_blocks.reshape(LENGTH, RANK)
    return grad_queries, grad_low_rank, grad_adapter
```

```python
import functools

import jax
import jax.numpy as jnp
from jax import lax
from jax.experimental import pallas as pl
from jax.experimental.pallas import tpu as pltpu
from jax.sharding import PartitionSpec as P

QH = 32
KVH = 4
HD = 128
RANK = 64
BLOCK = 128
CORES = 2
PAD = 16

adapter_scale_factor = 2.0
far_below = -1e30
logit_scale = HD ** (-0.5)
log2_scale = logit_scale * 1.4426950408889634

VMEM = pl.BlockSpec(memory_space=pltpu.VMEM)
SMEM = pl.BlockSpec(memory_space=pltpu.SMEM)
BF16 = jnp.bfloat16
F32 = jnp.float32


def pack_kernel(place, key_ref, value_ref, doc_ref, *refs):
    n = (len(refs) - 2) // 2
    b_refs, message, doc_column, b_outs = refs[:n], refs[n], refs[n + 1], refs[n + 2 :]
    tokens = key_ref.shape[0]
    message[:tokens, :HD] = key_ref[...]
    message[:tokens, HD:] = value_ref[...]
    docs = doc_ref[...].astype(F32)
    message[tokens:, :] = jnp.broadcast_to(docs, (PAD, tokens)).astype(BF16)
    row = lax.broadcasted_iota(jnp.int32, (tokens, tokens), 0)
    lane = lax.broadcasted_iota(jnp.int32, (tokens, tokens), 1)
    column = jnp.sum(jnp.where(row == lane, docs, 0.0), axis=1, keepdims=True)
    doc_column[...] = jnp.broadcast_to(column, doc_column.shape)
    for b_ref, b_out in zip(b_refs, b_outs):
        b_out[...] = b_ref[0]


def pack(place, keys, values, docs, adapter_b, owners, heads_dev):
    tokens = keys.shape[0]
    width = heads_dev * HD
    kv = lambda place: place[2] * heads_dev // (QH // KVH)
    return pl.pallas_call(
        pack_kernel,
        grid_spec=pltpu.PrefetchScalarGridSpec(
            num_scalar_prefetch=1,
            grid=(1,),
            in_specs=[
                pl.BlockSpec((tokens, HD), lambda i, place: (0, kv(place))),
                pl.BlockSpec((tokens, HD), lambda i, place: (0, kv(place))),
                pl.BlockSpec((1, tokens), lambda i, place: (0, 0)),
            ]
            + [
                pl.BlockSpec(
                    (1, RANK, width), lambda i, place, s=s: (0, 0, lax.rem(place[2] + s, owners))
                )
                for s in range(owners)
            ],
            out_specs=[
                pl.BlockSpec((tokens + PAD, 2 * HD), lambda i, place: (0, 0)),
                pl.BlockSpec((tokens, 128), lambda i, place: (0, 0)),
            ]
            + [pl.BlockSpec((RANK, width), lambda i, place: (0, 0))] * owners,
        ),
        out_shape=[
            jax.ShapeDtypeStruct((tokens + PAD, 2 * HD), BF16),
            jax.ShapeDtypeStruct((tokens, 128), F32),
        ]
        + [jax.ShapeDtypeStruct((RANK, width), BF16)] * owners,
        cost_estimate=pl.CostEstimate(flops=0, bytes_accessed=2 << 20, transcendentals=0),
        name="pack",
    )(place, keys, values, docs.reshape(1, tokens), *([adapter_b] * owners))


def lanes(x, times):
    return jnp.concatenate([x] * times, axis=1)


def attend_kernel(chips, owners, place, tenant, *refs):
    refs = list(refs)
    take = lambda count: [refs.pop(0) for _ in range(count)]
    (q_ref, g_ref, doc_column, low_ref) = take(4)
    own, other = take(chips), take(chips)
    b_refs = take(owners)
    (dq_ref,) = take(1)
    rank_outs = take(owners)
    mine_ref, partner_ref = take(2)
    top, by_key, by_grad, bias, chosen, rank_all = take(6)
    tokens, width = q_ref.shape
    heads = width // HD
    z, core, adp = place[0], place[1], place[2]
    doc_row = lambda ref: ref[tokens : tokens + PAD, :][:1].astype(F32)
    first_doc = jnp.min(doc_row(own[0]))
    query_doc = lanes(doc_column[...], 2 * tokens // 128)

    def step(shift):
        keys = jnp.concatenate([own[shift][:tokens, :HD], other[shift][:tokens, :HD]], axis=0)
        values = jnp.concatenate([own[shift][:tokens, HD:], other[shift][:tokens, HD:]], axis=0)
        extended = jnp.concatenate([keys, jnp.ones((2 * tokens, HD), BF16)], axis=1)
        other_doc = doc_row(other[shift])
        if shift == 0:
            other_doc = jnp.where(core == 1, other_doc, -1.0)
        visible = jnp.concatenate([doc_row(own[shift]), other_doc], axis=1) == query_doc
        if shift == 0:
            row = lax.broadcasted_iota(jnp.int32, (tokens, 2 * tokens), 0)
            lane = lax.broadcasted_iota(jnp.int32, (tokens, 2 * tokens), 1)
            visible = visible & ((lane <= row) | (lane >= tokens))
        bias[...] = jnp.where(visible, 0.0, far_below)
        for h in range(heads):
            columns = slice(h * HD, (h + 1) * HD)
            scores = (
                lax.dot_general(
                    q_ref[:, columns], keys, (((1,), (1,)), ((), ())), preferred_element_type=F32
                )
                + bias[...]
            )
            block_top = jnp.broadcast_to(jnp.max(scores, axis=1, keepdims=True), (tokens, 128))
            new_top = block_top if shift == 0 else jnp.maximum(top[h], block_top)
            p = jnp.exp2((scores - lanes(new_top, 2 * tokens // 128)) * log2_scale)
            grads = lax.dot_general(
                g_ref[:, columns], values, (((1,), (1,)), ((), ())), preferred_element_type=F32
            )
            key_sum = jnp.dot(p.astype(BF16), extended, preferred_element_type=F32)
            grad_sum = jnp.dot((p * grads).astype(BF16), extended, preferred_element_type=F32)
            if shift:
                decay = lanes(jnp.exp2((top[h] - new_top) * log2_scale), 2)
                key_sum = key_sum + by_key[h] * decay
                grad_sum = grad_sum + by_grad[h] * decay
            top[h] = new_top
            by_key[h] = key_sum
            by_grad[h] = grad_sum

    step(0)
    for shift in range(1, chips):
        latest = jnp.maximum(jnp.max(doc_row(own[shift])), jnp.max(doc_row(other[shift])))
        pl.when((z >= shift) & (latest == first_doc))(functools.partial(step, shift))

    for h in range(heads):
        columns = slice(h * HD, (h + 1) * HD)
        inverse = 1.0 / by_key[h, :, HD:]
        delta = by_grad[h, :, HD:] * inverse
        dq = (by_grad[h, :, :HD] - delta * by_key[h, :, :HD]) * (inverse * logit_scale)
        dq_ref[:, columns] = dq.astype(BF16)

    half = width // CORES
    for block in range(tokens // BLOCK):
        rows = slice(block * BLOCK, (block + 1) * BLOCK)
        holder = lax.rem(adp - tenant[block] + owners, owners)
        for s in range(owners):

            @pl.when(holder == s)
            def _(s=s):
                chosen[...] = b_refs[s][...]

        rank_all[rows, :] = adapter_scale_factor * lax.dot_general(
            dq_ref[rows, :], chosen[...], (((1,), (1,)), ((), ())), preferred_element_type=F32
        )
        partial = adapter_scale_factor * lax.dot_general(
            low_ref[rows, :], dq_ref[rows, :], (((0,), (0,)), ((), ())), preferred_element_type=F32
        )
        out_rows = slice(block * RANK, (block + 1) * RANK)
        mine_ref[out_rows, :] = jnp.where(core == 0, partial[:, :half], partial[:, half:])
        partner_ref[out_rows, :] = jnp.where(
            core == 0, partial[:, half:], partial[:, :half]
        ).astype(BF16)
    share = tokens // owners
    for s in range(owners):
        start = pl.multiple_of(lax.rem(adp + s, owners) * share, share)
        rank_outs[s][...] = rank_all[pl.ds(start, share), :]


def attend(place, block_tenant, queries, grad_out, doc_column, low_rank, own, other, b_cols):
    tokens, width = queries.shape
    heads = width // HD
    chips, owners = len(own), len(b_cols)
    blocks = tokens // BLOCK
    share = tokens // owners
    inputs = [queries, grad_out, doc_column, low_rank, *own, *other, *b_cols]
    return pl.pallas_call(
        functools.partial(attend_kernel, chips, owners),
        in_specs=[SMEM, SMEM] + [VMEM] * len(inputs),
        out_specs=[VMEM] * (3 + owners),
        out_shape=[jax.ShapeDtypeStruct((tokens, width), BF16)]
        + [jax.ShapeDtypeStruct((share, RANK), F32)] * owners
        + [
            jax.ShapeDtypeStruct((blocks * RANK, width // CORES), F32),
            jax.ShapeDtypeStruct((blocks * RANK, width // CORES), BF16),
        ],
        scratch_shapes=[
            pltpu.VMEM((heads, tokens, 128), F32),
            pltpu.VMEM((heads, tokens, 2 * HD), F32),
            pltpu.VMEM((heads, tokens, 2 * HD), F32),
            pltpu.VMEM((tokens, 2 * tokens), F32),
            pltpu.VMEM((RANK, width), BF16),
            pltpu.VMEM((tokens, RANK), F32),
        ],
        compiler_params=pltpu.CompilerParams(vmem_limit_bytes=40 << 20),
        cost_estimate=pl.CostEstimate(
            flops=chips * 12 * tokens * tokens * width, bytes_accessed=4 << 20, transcendentals=0
        ),
        name="attend",
    )(place, block_tenant, *inputs)


def tenants_kernel(owners, place, tenant, other_tenant, mine_ref, other_ref, *outs):
    blocks = mine_ref.shape[0] // RANK
    z, adp = place[0], place[2]
    for s in range(owners):
        owner = lax.rem(adp + z + s, owners)
        total = None
        for block in range(blocks):
            rows = slice(block * RANK, (block + 1) * RANK)
            term = jnp.where(tenant[block] == owner, mine_ref[rows, :], 0.0)
            total = term if total is None else total + term
            total = total + jnp.where(
                other_tenant[block] == owner, other_ref[rows, :].astype(F32), 0.0
            )
        outs[s][...] = total.astype(BF16)


def by_tenant(place, tenant, other_tenant, mine, other, owners):
    return pl.pallas_call(
        functools.partial(tenants_kernel, owners),
        in_specs=[SMEM] * 3 + [VMEM] * 2,
        out_specs=[VMEM] * owners,
        out_shape=[jax.ShapeDtypeStruct((RANK, mine.shape[1]), BF16)] * owners,
        cost_estimate=pl.CostEstimate(flops=0, bytes_accessed=1 << 20, transcendentals=0),
        name="by_tenant",
    )(place, tenant, other_tenant, mine, other)


def on_device(queries, keys, values, grad_out, docs, block_tenant, low_rank, adapter_b):
    positions, owners = lax.axis_size("ctx"), lax.axis_size("adp")
    chips = positions // CORES
    heads_dev = queries.shape[1] // HD
    ctx, adp = lax.axis_index("ctx"), lax.axis_index("adp")
    place = jnp.stack([ctx // CORES, ctx % CORES, adp]).astype(jnp.int32)
    swap = [(c, c ^ 1) for c in range(positions)]
    up = lambda s: [(c, (c + CORES * s) % positions) for c in range(positions)]
    along = lambda s: [(a, (a + s) % owners) for a in range(owners)]

    message, doc_column, *b_out = pack(
        place, keys, values, docs, adapter_b, owners, heads_dev
    )
    own = [message] + [lax.ppermute(message, "ctx", up(s)) for s in range(1, chips)]
    other = [lax.ppermute(m, "ctx", swap) for m in own]
    other_tenant = lax.ppermute(block_tenant, "ctx", swap)
    b_cols = [b_out[0]] + [lax.ppermute(b_out[s], "adp", along(s)) for s in range(1, owners)]

    grad_queries, *ranks, mine, partner = attend(
        place, block_tenant, queries, grad_out, doc_column, low_rank, own, other, b_cols
    )
    other_part = lax.ppermute(partner, "ctx", swap)
    pieces = by_tenant(place, block_tenant, other_tenant, mine, other_part, owners)

    def sideways(s):
        return [
            ((CORES * z + k) * owners + a, (CORES * z + k) * owners + (a + z + s) % owners)
            for z in range(chips)
            for k in range(CORES)
            for a in range(owners)
        ]

    def upright(s):
        return [
            ((CORES * z + k) * owners + t, (CORES * ((t - z - s) % owners) + k) * owners + t)
            for z in range(chips)
            for k in range(CORES)
            for t in range(owners)
        ]

    both = ("ctx", "adp")
    moved = [lax.ppermute(piece, both, sideways(s)) for s, piece in enumerate(pieces)]
    moved = [lax.ppermute(piece, both, upright(s)) for s, piece in enumerate(moved)]
    grad_adapter = sum(piece.astype(F32) for piece in moved)[None]
    ranks = [ranks[0]] + [lax.ppermute(ranks[s], "adp", along(s)) for s in range(1, owners)]
    return grad_queries, sum(ranks), grad_adapter


def solution(mesh):
    placed = (
        P("ctx", "adp"),
        P("ctx", None),
        P("ctx", None),
        P("ctx", "adp"),
        P("ctx"),
        P("ctx"),
        P("ctx", None),
        P("adp", None, None),
    )
    return jax.shard_map(
        on_device,
        mesh=mesh,
        in_specs=placed,
        out_specs=(P("ctx", "adp"), P(("ctx", "adp"), None), P("adp", None, "ctx")),
        check_vma=False,
    )
```

```python
import functools

import jax
import jax.numpy as jnp
from jax import lax
from jax.experimental import pallas as pl
from jax.experimental.pallas import tpu as pltpu
from jax.sharding import PartitionSpec as P

QH = 32
KVH = 4
HD = 128
RANK = 64
BLOCK = 128
CORES = 2
PAD = 16
GROUP = 4

adapter_scale_factor = 2.0
far_below = -1e30
logit_scale = HD ** (-0.5)
log2_scale = logit_scale * 1.4426950408889634

VMEM = pl.BlockSpec(memory_space=pltpu.VMEM)
SMEM = pl.BlockSpec(memory_space=pltpu.SMEM)
ANY = pl.BlockSpec(memory_space=pl.ANY)
HBM = pl.BlockSpec(memory_space=pltpu.HBM)
BF16 = jnp.bfloat16
F32 = jnp.float32


def small(bytes_accessed):
    return dict(
        compiler_params=pltpu.CompilerParams(vmem_limit_bytes=8 << 20),
        cost_estimate=pl.CostEstimate(flops=0, bytes_accessed=bytes_accessed, transcendentals=0),
    )


def pack_kernel(heads_dev, tenant_hbm, keys, values, docs_hbm, message, tenant, docs, sems):
    tokens = keys.shape[0]
    kv = lax.axis_index("adp") * heads_dev // (QH // KVH)
    head = pl.ds(pl.multiple_of(kv * HD, HD), HD)
    copies = [
        pltpu.make_async_copy(docs_hbm, docs, sems.at[0]),
        pltpu.make_async_copy(tenant_hbm, tenant, sems.at[1]),
        pltpu.make_async_copy(keys.at[:, head], message.at[pl.ds(0, tokens), pl.ds(0, HD)], sems.at[2]),
        pltpu.make_async_copy(values.at[:, head], message.at[pl.ds(0, tokens), pl.ds(HD, HD)], sems.at[3]),
    ]
    for copy in copies:
        copy.start()
    for copy in copies[:2]:
        copy.wait()
    row = lax.broadcasted_iota(jnp.int32, (PAD, tokens), 0)
    told = jnp.broadcast_to(docs[...].astype(F32), (PAD, tokens))
    for block in range(tokens // BLOCK):
        told = jnp.where(row == 1 + block, tenant[block].astype(F32), told)
    message[tokens:, :] = told.astype(BF16)
    for copy in copies[2:]:
        copy.wait()


def pack(block_tenant, keys, values, docs, heads_dev):
    tokens = keys.shape[0]
    return pl.pallas_call(
        functools.partial(pack_kernel, heads_dev),
        in_specs=[HBM] * 4,
        out_specs=VMEM,
        out_shape=jax.ShapeDtypeStruct((tokens + PAD, 2 * HD), BF16),
        scratch_shapes=[
            pltpu.SMEM(block_tenant.shape, jnp.int32),
            pltpu.VMEM((1, tokens), jnp.int32),
            pltpu.SemaphoreType.DMA((4,)),
        ],
        name="pack",
        **small(1 << 18),
    )(block_tenant, keys, values, docs.reshape(1, tokens))


def columns_kernel(owners, adapter_b, after, *refs):
    outs, sems = refs[:owners], refs[owners]
    width = outs[0].shape[1]
    adp = lax.axis_index("adp")
    copies = []
    for s in range(owners):
        start = pl.multiple_of(lax.rem(adp + s, owners) * width, 128)
        copies.append(pltpu.make_async_copy(adapter_b.at[0, :, pl.ds(start, width)], outs[s], sems.at[s]))
        copies[-1].start()
    for copy in copies:
        copy.wait()


def columns(adapter_b, after, owners):
    width = adapter_b.shape[2] // owners
    return pl.pallas_call(
        functools.partial(columns_kernel, owners),
        in_specs=[ANY, ANY],
        out_specs=[VMEM] * owners,
        out_shape=[jax.ShapeDtypeStruct((RANK, width), BF16)] * owners,
        scratch_shapes=[pltpu.SemaphoreType.DMA((owners,))],
        name="columns",
        **small(1 << 19),
    )(adapter_b, after)


def lanes(x, times):
    return jnp.concatenate([x] * times, axis=1)


def rows(x, times):
    return jnp.concatenate([x] * times, axis=0)


def attend_kernel(shifts, first, last, *refs):
    refs = list(refs)
    take = lambda count: [refs.pop(0) for _ in range(count)]
    q_ref, g_ref, docs_ref = take(3)
    own, other = take(len(shifts)), take(len(shifts))
    if not first:
        top_in, by_key_in, by_grad_in = take(3)
    if last:
        low_ref, dq_ref, mine_ref, partner_ref = take(4)
    top, by_key, by_grad, bias = take(4)
    tokens, width = q_ref.shape
    heads = width // HD
    group = min(GROUP, heads)
    ctx = lax.axis_index("ctx")
    z, core = ctx // CORES, lax.rem(ctx, CORES)
    doc_row = lambda ref: ref[tokens : tokens + PAD, :][:1].astype(F32)

    docs = doc_row(docs_ref)
    first_doc = jnp.min(docs)
    row = lax.broadcasted_iota(jnp.int32, (tokens, tokens), 0)
    lane = lax.broadcasted_iota(jnp.int32, (tokens, tokens), 1)
    doc_column = jnp.sum(jnp.where(row == lane, docs, 0.0), axis=1, keepdims=True)

    def stacked(ref, h):
        return jnp.concatenate(
            [ref[:, i * HD : (i + 1) * HD] for i in range(h, h + group)], axis=0
        )

    def step(index, shift, old):
        keys = jnp.concatenate([own[index][:tokens, :HD], other[index][:tokens, :HD]], axis=0)
        values = jnp.concatenate([own[index][:tokens, HD:], other[index][:tokens, HD:]], axis=0)
        extended = jnp.concatenate([keys, jnp.ones((2 * tokens, HD), BF16)], axis=1)
        own_seen = doc_row(own[index]) == doc_column
        other_doc = doc_row(other[index])
        if shift == 0:
            own_seen = own_seen & (lane <= row)
            other_doc = jnp.where(core == 1, other_doc, -1.0)
        other_seen = other_doc == doc_column
        bias[:, :tokens] = jnp.where(own_seen, 0.0, far_below)
        bias[:, tokens:] = jnp.where(other_seen, 0.0, far_below)
        for h in range(0, heads, group):
            part = slice(h * tokens, (h + group) * tokens)
            scores = lax.dot_general(
                stacked(q_ref, h), keys, (((1,), (1,)), ((), ())), preferred_element_type=F32
            ) + rows(bias[...], group)
            block_top = jnp.broadcast_to(
                jnp.max(scores, axis=1, keepdims=True), (group * tokens, 128)
            )
            new_top = block_top if shift == 0 else jnp.maximum(old[0][part, :], block_top)
            p = jnp.exp2((scores - lanes(new_top, 2 * tokens // 128)) * log2_scale)
            grads = lax.dot_general(
                stacked(g_ref, h), values, (((1,), (1,)), ((), ())), preferred_element_type=F32
            )
            key_sum = jnp.dot(p.astype(BF16), extended, preferred_element_type=F32)
            grad_sum = jnp.dot((p * grads).astype(BF16), extended, preferred_element_type=F32)
            if shift:
                decay = lanes(jnp.exp2((old[0][part, :] - new_top) * log2_scale), 2)
                key_sum = key_sum + old[1][part, :] * decay
                grad_sum = grad_sum + old[2][part, :] * decay
            top[part, :] = new_top
            by_key[part, :] = key_sum
            by_grad[part, :] = grad_sum

    for index, shift in enumerate(shifts):
        if shift == 0:
            step(index, shift, None)
            continue
        old = (top, by_key, by_grad)
        latest = jnp.max(jnp.maximum(doc_row(own[index]), doc_row(other[index])))
        needed = (z >= shift) & (latest == first_doc)
        if index == 0:
            old = (top_in, by_key_in, by_grad_in)

            @pl.when(jnp.logical_not(needed))
            def _():
                for kept, given in zip((top, by_key, by_grad), old):
                    kept[...] = given[...]

        pl.when(needed)(functools.partial(step, index, shift, old))

    if not last:
        return
    for h in range(heads):
        part = slice(h * tokens, (h + 1) * tokens)
        inverse = 1.0 / by_key[part, HD:]
        delta = by_grad[part, HD:] * inverse
        dq = (by_grad[part, :HD] - delta * by_key[part, :HD]) * (inverse * logit_scale)
        dq_ref[:, h * HD : (h + 1) * HD] = dq.astype(BF16)

    half = width // CORES
    for block in range(tokens // BLOCK):
        block_rows = slice(block * BLOCK, (block + 1) * BLOCK)
        partial = adapter_scale_factor * jnp.dot(
            low_ref[:, block_rows], dq_ref[block_rows, :], preferred_element_type=F32
        )
        out_rows = slice(block * RANK, (block + 1) * RANK)
        mine_ref[out_rows, :] = jnp.where(core == 0, partial[:, :half], partial[:, half:])
        partner_ref[out_rows, :] = jnp.where(
            core == 0, partial[:, half:], partial[:, :half]
        ).astype(BF16)


def attend(shifts, queries, grad_out, message, own, other, state=None, low_rank=None):
    tokens, width = queries.shape
    heads = width // HD
    blocks = tokens // BLOCK
    sums = [
        ((heads * tokens, 128), F32),
        ((heads * tokens, 2 * HD), F32),
        ((heads * tokens, 2 * HD), F32),
    ]
    inputs = [queries, grad_out, message, *own, *other]
    scratch = [pltpu.VMEM((tokens, 2 * tokens), F32)]
    if state is not None:
        inputs += state
    if low_rank is None:
        outs = sums
    else:
        inputs.append(low_rank.T)
        scratch = [pltpu.VMEM(*each) for each in sums] + scratch
        outs = [
            ((tokens, width), BF16),
            ((blocks * RANK, width // CORES), F32),
            ((blocks * RANK, width // CORES), BF16),
        ]
    return pl.pallas_call(
        functools.partial(attend_kernel, shifts, state is None, low_rank is not None),
        in_specs=[VMEM] * len(inputs),
        out_specs=[VMEM] * len(outs),
        out_shape=[jax.ShapeDtypeStruct(*each) for each in outs],
        scratch_shapes=scratch,
        compiler_params=pltpu.CompilerParams(vmem_limit_bytes=30 << 20),
        cost_estimate=pl.CostEstimate(
            flops=len(shifts) * 12 * tokens * tokens * width,
            bytes_accessed=4 << 20,
            transcendentals=0,
        ),
        name="attend_" + "_".join(map(str, shifts[:4])),
    )(*inputs)


def ranks_kernel(owners, tenant_hbm, dq_ref, *refs):
    b_refs, rank_ref, chosen, tenant, sem = refs[:owners], *refs[owners:]
    copy = pltpu.make_async_copy(tenant_hbm, tenant, sem)
    copy.start()
    copy.wait()
    adp = lax.axis_index("adp")
    for block in range(dq_ref.shape[0] // BLOCK):
        block_rows = slice(block * BLOCK, (block + 1) * BLOCK)
        holder = lax.rem(adp - tenant[block] + owners, owners)
        for s in range(owners):

            @pl.when(holder == s)
            def _(s=s):
                chosen[...] = b_refs[s][...]

        rank_ref[block_rows, :] = adapter_scale_factor * lax.dot_general(
            dq_ref[block_rows, :], chosen[...], (((1,), (1,)), ((), ())), preferred_element_type=F32
        )


def ranks_of(tenant, dq, b_cols):
    tokens, width = dq.shape
    return pl.pallas_call(
        functools.partial(ranks_kernel, len(b_cols)),
        in_specs=[HBM] + [VMEM] * (1 + len(b_cols)),
        out_specs=VMEM,
        out_shape=jax.ShapeDtypeStruct((tokens, RANK), F32),
        scratch_shapes=[
            pltpu.VMEM((RANK, width), BF16),
            pltpu.SMEM(tenant.shape, jnp.int32),
            pltpu.SemaphoreType.DMA,
        ],
        name="ranks",
        **small(1 << 20),
    )(tenant, dq, *b_cols)


def tenants_kernel(owners, mine_ref, other_ref, own_notes, other_notes, rank_ref, *outs):
    blocks = mine_ref.shape[0] // RANK
    width = mine_ref.shape[1]
    share = rank_ref.shape[0] // owners
    adp = lax.axis_index("adp")
    told = [ref[ref.shape[0] - PAD :, :HD].astype(F32) for ref in (own_notes, other_notes)]
    for s in range(owners):
        owner = lax.rem(adp + s, owners)
        total = jnp.zeros((RANK, width), F32)
        for block in range(blocks):
            part = slice(block * RANK, (block + 1) * RANK)
            for each, ref in zip(told, (mine_ref, other_ref)):
                chosen = lanes(each[1 + block : 2 + block] == owner.astype(F32), width // HD)
                total = total + jnp.where(chosen, ref[part, :].astype(F32), 0.0)
        outs[s][:RANK, :] = total.astype(BF16)
        outs[s][RANK:, :] = jnp.zeros((PAD, width), BF16)
        for part in range(share // PAD):
            start = pl.multiple_of(owner * share + part * PAD, PAD)
            outs[s][RANK:, part * HD : part * HD + RANK] = rank_ref[pl.ds(start, PAD), :].astype(BF16)


def by_tenant(mine, other, own_message, other_message, ranks, owners):
    width = mine.shape[1]
    return pl.pallas_call(
        functools.partial(tenants_kernel, owners),
        in_specs=[VMEM] * 5,
        out_specs=[VMEM] * owners,
        out_shape=[jax.ShapeDtypeStruct((RANK + PAD, width), BF16)] * owners,
        name="by_tenant",
        **small(1 << 20),
    )(mine, other, own_message, other_message, ranks)


def columns_owner_kernel(owners, *refs):
    pieces, outs, rank_out = refs[:owners], refs[owners:-1], refs[-1]
    ctx, adp = lax.axis_index("ctx"), lax.axis_index("adp")
    z = ctx // CORES
    share = rank_out.shape[0]
    for part in range(share // PAD):
        rank_out[part * PAD : (part + 1) * PAD, :] = sum(
            piece[RANK:, part * HD : part * HD + RANK].astype(F32) for piece in pieces
        )
    for s in range(owners):
        source = lax.rem(adp - z - s + 2 * owners, owners)
        for j in range(owners):

            @pl.when(source == j)
            def _(s=s, j=j):
                outs[s][...] = pieces[j][:RANK, :]


def by_columns_owner(pieces, share):
    owners = len(pieces)
    width = pieces[0].shape[1]
    return pl.pallas_call(
        functools.partial(columns_owner_kernel, owners),
        in_specs=[VMEM] * owners,
        out_specs=[VMEM] * (owners + 1),
        out_shape=[jax.ShapeDtypeStruct((RANK, width), BF16)] * owners
        + [jax.ShapeDtypeStruct((share, RANK), F32)],
        name="by_columns_owner",
        **small(1 << 20),
    )(*pieces)


def on_device(queries, keys, values, grad_out, docs, block_tenant, low_rank, adapter_b):
    positions, owners = lax.axis_size("ctx"), lax.axis_size("adp")
    chips = positions // CORES
    tokens = queries.shape[0]
    heads_dev = queries.shape[1] // HD
    swap = [(c, c ^ 1) for c in range(positions)]
    up = lambda s: [(c, (c + CORES * s) % positions) for c in range(positions)]
    along = lambda s: [(a, (a + s) % owners) for a in range(owners)]

    message = pack(block_tenant, keys, values, docs, heads_dev)
    own = [message] + [lax.ppermute(message, "ctx", up(s)) for s in range(1, chips)]
    other = [lax.ppermute(message, "ctx", swap)]
    b_out = columns(adapter_b, other[0], owners)
    b_cols = [b_out[0]] + [lax.ppermute(b_out[s], "adp", along(s)) for s in range(1, owners)]
    state = attend((0,), queries, grad_out, message, own[:1], other[:1])
    own, state, b_cols = lax.optimization_barrier((own, state, b_cols))
    other += [lax.ppermute(m, "ctx", swap) for m in own[1:]]

    grad_queries, mine, partner = attend(
        tuple(range(1, chips)), queries, grad_out, message, own[1:], other[1:], state, low_rank
    )
    other_part = lax.ppermute(partner, "ctx", swap)
    ranks = ranks_of(block_tenant, grad_queries, b_cols)
    pieces = by_tenant(mine, other_part, message, other[0], ranks, owners)
    pieces = [pieces[0]] + [
        lax.ppermute(pieces[s], "adp", along(s)) for s in range(1, owners)
    ]
    *pieces, grad_low_rank = by_columns_owner(pieces, tokens // owners)
    pieces = [pieces[0]] + [lax.ppermute(pieces[s], "ctx", up(s)) for s in range(1, chips)]
    grad_adapter = sum(piece.astype(F32) for piece in pieces)[None]
    return grad_queries, grad_low_rank, grad_adapter


def solution(mesh):
    placed = (
        P("ctx", "adp"),
        P("ctx", None),
        P("ctx", None),
        P("ctx", "adp"),
        P("ctx"),
        P("ctx"),
        P("ctx", None),
        P("adp", None, None),
    )
    return jax.shard_map(
        on_device,
        mesh=mesh,
        in_specs=placed,
        out_specs=(P("ctx", "adp"), P(("ctx", "adp"), None), P("adp", None, "ctx")),
        check_vma=False,
    )
```

```python
import functools

import jax
import jax.numpy as jnp
from jax import lax
from jax.experimental import pallas as pl
from jax.experimental.pallas import tpu as pltpu
from jax.sharding import PartitionSpec as P

QH = 32
KVH = 4
HD = 128
RANK = 64
BLOCK = 128
CORES = 2
PAD = 16
GROUP = 4
PACK_LIMIT = (64 << 20) - (1 << 18)

adapter_scale_factor = 2.0
far_below = -1e30
logit_scale = HD ** (-0.5)
log2_scale = logit_scale * 1.4426950408889634

VMEM = pl.BlockSpec(memory_space=pltpu.VMEM)
SMEM = pl.BlockSpec(memory_space=pltpu.SMEM)
ANY = pl.BlockSpec(memory_space=pl.ANY)
HBM = pl.BlockSpec(memory_space=pltpu.HBM)
BF16 = jnp.bfloat16
F32 = jnp.float32


def small(bytes_accessed):
    return dict(
        compiler_params=pltpu.CompilerParams(vmem_limit_bytes=8 << 20),
        cost_estimate=pl.CostEstimate(flops=0, bytes_accessed=bytes_accessed, transcendentals=0),
    )


def pack_kernel(heads_dev, tenant_hbm, keys, values, docs_hbm, message, tenant, docs, sems):
    tokens = keys.shape[0]
    kv = lax.axis_index("adp") * heads_dev // (QH // KVH)
    head = pl.ds(pl.multiple_of(kv * HD, HD), HD)
    copies = [
        pltpu.make_async_copy(docs_hbm, docs, sems.at[0]),
        pltpu.make_async_copy(tenant_hbm, tenant, sems.at[1]),
        pltpu.make_async_copy(keys.at[:, head], message.at[pl.ds(0, tokens), pl.ds(0, HD)], sems.at[2]),
        pltpu.make_async_copy(values.at[:, head], message.at[pl.ds(0, tokens), pl.ds(HD, HD)], sems.at[3]),
    ]
    for copy in copies:
        copy.start()
    for copy in copies[:2]:
        copy.wait()
    row = lax.broadcasted_iota(jnp.int32, (PAD, tokens), 0)
    told = jnp.broadcast_to(docs[...].astype(F32), (PAD, tokens))
    for block in range(tokens // BLOCK):
        told = jnp.where(row == 1 + block, tenant[block].astype(F32), told)
    message[tokens:, :] = told.astype(BF16)
    for copy in copies[2:]:
        copy.wait()


def pack(block_tenant, keys, values, docs, heads_dev):
    tokens = keys.shape[0]
    return pl.pallas_call(
        functools.partial(pack_kernel, heads_dev),
        in_specs=[HBM] * 4,
        out_specs=VMEM,
        out_shape=jax.ShapeDtypeStruct((tokens + PAD, 2 * HD), BF16),
        scratch_shapes=[
            pltpu.SMEM(block_tenant.shape, jnp.int32),
            pltpu.VMEM((1, tokens), jnp.int32),
            pltpu.SemaphoreType.DMA((4,)),
        ],
        name="pack",
        compiler_params=pltpu.CompilerParams(vmem_limit_bytes=PACK_LIMIT),
        cost_estimate=pl.CostEstimate(flops=0, bytes_accessed=1 << 18, transcendentals=0),
    )(block_tenant, keys, values, docs.reshape(1, tokens))


def columns_kernel(owners, adapter_b, after, *refs):
    outs, sems = refs[:owners], refs[owners]
    width = outs[0].shape[1]
    adp = lax.axis_index("adp")
    copies = []
    for s in range(owners):
        start = pl.multiple_of(lax.rem(adp + s, owners) * width, 128)
        copies.append(pltpu.make_async_copy(adapter_b.at[0, :, pl.ds(start, width)], outs[s], sems.at[s]))
        copies[-1].start()
    for copy in copies:
        copy.wait()


def columns(adapter_b, after, owners):
    width = adapter_b.shape[2] // owners
    return pl.pallas_call(
        functools.partial(columns_kernel, owners),
        in_specs=[ANY, ANY],
        out_specs=[VMEM] * owners,
        out_shape=[jax.ShapeDtypeStruct((RANK, width), BF16)] * owners,
        scratch_shapes=[pltpu.SemaphoreType.DMA((owners,))],
        name="columns",
        compiler_params=pltpu.CompilerParams(vmem_limit_bytes=8 << 20),
        cost_estimate=pl.CostEstimate(flops=1 << 33, bytes_accessed=1 << 19, transcendentals=0),
    )(adapter_b, after)


def lanes(x, times):
    return jnp.concatenate([x] * times, axis=1)


def rows(x, times):
    return jnp.concatenate([x] * times, axis=0)


def attend_kernel(shifts, first, last, owners, *refs):
    refs = list(refs)
    take = lambda count: [refs.pop(0) for _ in range(count)]
    q_ref, g_ref, docs_ref = take(3)
    own, other = take(len(shifts)), take(len(shifts))
    if not first:
        top_in, by_key_in, by_grad_in = take(3)
    if last:
        (low_ref,) = take(1)
        b_refs = take(owners)
        dq_hbm, rank_ref, mine_ref, partner_ref = take(4)
    top, by_key, by_grad, bias = take(4)
    if last:
        dq_ref, chosen, dq_sem = take(3)
    tokens, width = q_ref.shape
    heads = width // HD
    group = min(GROUP, heads)
    ctx = lax.axis_index("ctx")
    z, core = ctx // CORES, lax.rem(ctx, CORES)
    doc_row = lambda ref: ref[tokens : tokens + PAD, :][:1].astype(F32)

    docs = doc_row(docs_ref)
    first_doc = jnp.min(docs)
    row = lax.broadcasted_iota(jnp.int32, (tokens, tokens), 0)
    lane = lax.broadcasted_iota(jnp.int32, (tokens, tokens), 1)
    doc_column = jnp.sum(jnp.where(row == lane, docs, 0.0), axis=1, keepdims=True)

    def stacked(ref, h):
        return jnp.concatenate(
            [ref[:, i * HD : (i + 1) * HD] for i in range(h, h + group)], axis=0
        )

    def step(index, shift, old):
        keys = jnp.concatenate([own[index][:tokens, :HD], other[index][:tokens, :HD]], axis=0)
        values = jnp.concatenate([own[index][:tokens, HD:], other[index][:tokens, HD:]], axis=0)
        extended = jnp.concatenate([keys, jnp.ones((2 * tokens, HD), BF16)], axis=1)
        own_seen = doc_row(own[index]) == doc_column
        other_doc = doc_row(other[index])
        if shift == 0:
            own_seen = own_seen & (lane <= row)
            other_doc = jnp.where(core == 1, other_doc, -1.0)
        other_seen = other_doc == doc_column
        bias[:, :tokens] = jnp.where(own_seen, 0.0, far_below)
        bias[:, tokens:] = jnp.where(other_seen, 0.0, far_below)
        for h in range(0, heads, group):
            part = slice(h * tokens, (h + group) * tokens)
            scores = lax.dot_general(
                stacked(q_ref, h), keys, (((1,), (1,)), ((), ())), preferred_element_type=F32
            ) + rows(bias[...], group)
            block_top = jnp.broadcast_to(
                jnp.max(scores, axis=1, keepdims=True), (group * tokens, 128)
            )
            new_top = block_top if shift == 0 else jnp.maximum(old[0][part, :], block_top)
            p = jnp.exp2((scores - lanes(new_top, 2 * tokens // 128)) * log2_scale)
            grads = lax.dot_general(
                stacked(g_ref, h), values, (((1,), (1,)), ((), ())), preferred_element_type=F32
            )
            key_sum = jnp.dot(p.astype(BF16), extended, preferred_element_type=F32)
            grad_sum = jnp.dot((p * grads).astype(BF16), extended, preferred_element_type=F32)
            if shift:
                decay = lanes(jnp.exp2((old[0][part, :] - new_top) * log2_scale), 2)
                key_sum = key_sum + old[1][part, :] * decay
                grad_sum = grad_sum + old[2][part, :] * decay
            top[part, :] = new_top
            by_key[part, :] = key_sum
            by_grad[part, :] = grad_sum

    for index, shift in enumerate(shifts):
        if shift == 0:
            step(index, shift, None)
            continue
        old = (top, by_key, by_grad)
        latest = jnp.max(jnp.maximum(doc_row(own[index]), doc_row(other[index])))
        needed = (z >= shift) & (latest == first_doc)
        if index == 0:
            old = (top_in, by_key_in, by_grad_in)

            @pl.when(jnp.logical_not(needed))
            def _():
                for kept, given in zip((top, by_key, by_grad), old):
                    kept[...] = given[...]

        pl.when(needed)(functools.partial(step, index, shift, old))

    if not last:
        return
    copies = []
    for h in range(heads):
        part = slice(h * tokens, (h + 1) * tokens)
        inverse = 1.0 / by_key[part, HD:]
        delta = by_grad[part, HD:] * inverse
        dq = (by_grad[part, :HD] - delta * by_key[part, :HD]) * (inverse * logit_scale)
        dq_ref[:, h * HD : (h + 1) * HD] = dq.astype(BF16)
        if (h + 1) % group == 0:
            columns = pl.ds((h + 1 - group) * HD, group * HD)
            copies.append(
                pltpu.make_async_copy(
                    dq_ref.at[:, columns], dq_hbm.at[:, columns], dq_sem.at[h // group]
                )
            )
            copies[-1].start()

    half = width // CORES
    adp = lax.axis_index("adp")
    told = docs_ref[tokens:, :HD].astype(F32)
    for block in range(tokens // BLOCK):
        block_rows = slice(block * BLOCK, (block + 1) * BLOCK)
        partial = adapter_scale_factor * jnp.dot(
            low_ref[:, block_rows], dq_ref[block_rows, :], preferred_element_type=F32
        )
        out_rows = slice(block * RANK, (block + 1) * RANK)
        mine_ref[out_rows, :] = jnp.where(core == 0, partial[:, :half], partial[:, half:])
        partner_ref[out_rows, :] = jnp.where(
            core == 0, partial[:, half:], partial[:, :half]
        ).astype(BF16)

        tenant = jnp.max(told[1 + block : 2 + block]).astype(jnp.int32)
        holder = lax.rem(adp - tenant + owners, owners)
        for s in range(owners):

            @pl.when(holder == s)
            def _(s=s):
                chosen[...] = b_refs[s][...]

        rank_ref[block_rows, :] = adapter_scale_factor * lax.dot_general(
            dq_ref[block_rows, :], chosen[...], (((1,), (1,)), ((), ())), preferred_element_type=F32
        )
    for copy in copies:
        copy.wait()


def attend(shifts, queries, grad_out, message, own, other, state=None, low_rank=None, b_cols=()):
    tokens, width = queries.shape
    heads = width // HD
    blocks = tokens // BLOCK
    sums = [
        ((heads * tokens, 128), F32),
        ((heads * tokens, 2 * HD), F32),
        ((heads * tokens, 2 * HD), F32),
    ]
    inputs = [queries, grad_out, message, *own, *other]
    scratch = [pltpu.VMEM((tokens, 2 * tokens), F32)]
    if state is not None:
        inputs += state
    if low_rank is None:
        outs = sums
    else:
        inputs += [low_rank.T, *b_cols]
        scratch = [pltpu.VMEM(*each) for each in sums] + scratch
        scratch += [
            pltpu.VMEM((tokens, width), BF16),
            pltpu.VMEM((RANK, width), BF16),
            pltpu.SemaphoreType.DMA((max(1, heads // GROUP),)),
        ]
        outs = [
            ((tokens, width), BF16),
            ((tokens, RANK), F32),
            ((blocks * RANK, width // CORES), F32),
            ((blocks * RANK, width // CORES), BF16),
        ]
    return pl.pallas_call(
        functools.partial(
            attend_kernel, shifts, state is None, low_rank is not None, len(b_cols)
        ),
        in_specs=[VMEM] * len(inputs),
        out_specs=([VMEM] if low_rank is None else [ANY]) + [VMEM] * (len(outs) - 1),
        out_shape=[jax.ShapeDtypeStruct(*each) for each in outs],
        scratch_shapes=scratch,
        compiler_params=pltpu.CompilerParams(vmem_limit_bytes=30 << 20),
        cost_estimate=pl.CostEstimate(
            flops=len(shifts) * 12 * tokens * tokens * width,
            bytes_accessed=4 << 20,
            transcendentals=0,
        ),
        name="attend_" + "_".join(map(str, shifts[:4])),
    )(*inputs)


def tenants_kernel(owners, mine_ref, other_ref, own_notes, other_notes, rank_ref, *outs):
    blocks = mine_ref.shape[0] // RANK
    width = mine_ref.shape[1]
    share = rank_ref.shape[0] // owners
    adp = lax.axis_index("adp")
    told = [ref[ref.shape[0] - PAD :, :HD].astype(F32) for ref in (own_notes, other_notes)]
    for s in range(owners):
        owner = lax.rem(adp + s, owners)
        total = jnp.zeros((RANK, width), F32)
        for block in range(blocks):
            part = slice(block * RANK, (block + 1) * RANK)
            for each, ref in zip(told, (mine_ref, other_ref)):
                chosen = lanes(each[1 + block : 2 + block] == owner.astype(F32), width // HD)
                total = total + jnp.where(chosen, ref[part, :].astype(F32), 0.0)
        outs[s][:RANK, :] = total.astype(BF16)
        outs[s][RANK:, :] = jnp.zeros((PAD, width), BF16)
        for part in range(share // PAD):
            start = pl.multiple_of(owner * share + part * PAD, PAD)
            outs[s][RANK:, part * HD : part * HD + RANK] = rank_ref[pl.ds(start, PAD), :].astype(BF16)


def by_tenant(mine, other, own_message, other_message, ranks, owners):
    width = mine.shape[1]
    return pl.pallas_call(
        functools.partial(tenants_kernel, owners),
        in_specs=[VMEM] * 5,
        out_specs=[VMEM] * owners,
        out_shape=[jax.ShapeDtypeStruct((RANK + PAD, width), BF16)] * owners,
        name="by_tenant",
        **small(1 << 20),
    )(mine, other, own_message, other_message, ranks)


def columns_owner_kernel(owners, *refs):
    pieces, outs, rank_out = refs[:owners], refs[owners:-1], refs[-1]
    ctx, adp = lax.axis_index("ctx"), lax.axis_index("adp")
    z = ctx // CORES
    share = rank_out.shape[0]
    for part in range(share // PAD):
        rank_out[part * PAD : (part + 1) * PAD, :] = sum(
            piece[RANK:, part * HD : part * HD + RANK].astype(F32) for piece in pieces
        )
    for s in range(owners):
        source = lax.rem(adp - z - s + 2 * owners, owners)
        for j in range(owners):

            @pl.when(source == j)
            def _(s=s, j=j):
                outs[s][...] = pieces[j][:RANK, :]


def by_columns_owner(pieces, share):
    owners = len(pieces)
    width = pieces[0].shape[1]
    return pl.pallas_call(
        functools.partial(columns_owner_kernel, owners),
        in_specs=[VMEM] * owners,
        out_specs=[VMEM] * (owners + 1),
        out_shape=[jax.ShapeDtypeStruct((RANK, width), BF16)] * owners
        + [jax.ShapeDtypeStruct((share, RANK), F32)],
        name="by_columns_owner",
        **small(1 << 20),
    )(*pieces)


def on_device(queries, keys, values, grad_out, docs, block_tenant, low_rank, adapter_b):
    positions, owners = lax.axis_size("ctx"), lax.axis_size("adp")
    chips = positions // CORES
    tokens = queries.shape[0]
    heads_dev = queries.shape[1] // HD
    swap = [(c, c ^ 1) for c in range(positions)]
    up = lambda s: [(c, (c + CORES * s) % positions) for c in range(positions)]
    along = lambda s: [(a, (a + s) % owners) for a in range(owners)]

    message = pack(block_tenant, keys, values, docs, heads_dev)
    far = {s: lax.ppermute(message, "ctx", up(s)) for s in reversed(range(1, chips))}
    own = [message] + [far[s] for s in range(1, chips)]
    other = [lax.ppermute(message, "ctx", swap)]
    b_out = columns(adapter_b, other[0], owners)
    b_cols = [b_out[0]] + [lax.ppermute(b_out[s], "adp", along(s)) for s in range(1, owners)]
    state = attend((0,), queries, grad_out, message, own[:1], other[:1])
    own[:3], state, b_cols = lax.optimization_barrier((own[:3], state, b_cols))
    other += [lax.ppermute(m, "ctx", swap) for m in own[1:]]
    grad_queries, ranks, mine, partner = attend(
        tuple(range(1, chips)),
        queries,
        grad_out,
        message,
        own[1:],
        other[1:],
        state,
        low_rank,
        b_cols,
    )
    other_part = lax.ppermute(partner, "ctx", swap)
    pieces = by_tenant(mine, other_part, message, other[0], ranks, owners)
    pieces = [pieces[0]] + [
        lax.ppermute(pieces[s], "adp", along(s)) for s in range(1, owners)
    ]
    *pieces, grad_low_rank = by_columns_owner(pieces, tokens // owners)
    pieces = [pieces[0]] + [lax.ppermute(pieces[s], "ctx", up(s)) for s in range(1, chips)]
    grad_adapter = sum(piece.astype(F32) for piece in pieces)[None]
    return grad_queries, grad_low_rank, grad_adapter


def solution(mesh):
    placed = (
        P("ctx", "adp"),
        P("ctx", None),
        P("ctx", None),
        P("ctx", "adp"),
        P("ctx"),
        P("ctx"),
        P("ctx", None),
        P("adp", None, None),
    )
    return jax.shard_map(
        on_device,
        mesh=mesh,
        in_specs=placed,
        out_specs=(P("ctx", "adp"), P(("ctx", "adp"), None), P("adp", None, "ctx")),
        check_vma=False,
    )
```

```python
import functools

import jax
import jax.numpy as jnp
from jax import lax
from jax.experimental import pallas as pl
from jax.experimental.pallas import tpu as pltpu
from jax.sharding import PartitionSpec as P

QH = 32
KVH = 4
HD = 128
RANK = 64
BLOCK = 128
CORES = 2
PAD = 16
GROUP = 4
PACK_LIMIT = (64 << 20) - (1 << 18)

adapter_scale_factor = 2.0
far_below = -1e30
logit_scale = HD ** (-0.5)
log2_scale = logit_scale * 1.4426950408889634

VMEM = pl.BlockSpec(memory_space=pltpu.VMEM)
SMEM = pl.BlockSpec(memory_space=pltpu.SMEM)
ANY = pl.BlockSpec(memory_space=pl.ANY)
HBM = pl.BlockSpec(memory_space=pltpu.HBM)
BF16 = jnp.bfloat16
F32 = jnp.float32


def small(bytes_accessed):
    return dict(
        compiler_params=pltpu.CompilerParams(vmem_limit_bytes=8 << 20),
        cost_estimate=pl.CostEstimate(flops=0, bytes_accessed=bytes_accessed, transcendentals=0),
    )


def pack_kernel(heads_dev, tenant_hbm, keys, values, docs_hbm, message, tenant, docs, sems):
    tokens = keys.shape[0]
    kv = lax.axis_index("adp") * heads_dev // (QH // KVH)
    head = pl.ds(pl.multiple_of(kv * HD, HD), HD)
    copies = [
        pltpu.make_async_copy(docs_hbm, docs, sems.at[0]),
        pltpu.make_async_copy(tenant_hbm, tenant, sems.at[1]),
        pltpu.make_async_copy(keys.at[:, head], message.at[pl.ds(0, tokens), pl.ds(0, HD)], sems.at[2]),
        pltpu.make_async_copy(values.at[:, head], message.at[pl.ds(0, tokens), pl.ds(HD, HD)], sems.at[3]),
    ]
    for copy in copies:
        copy.start()
    for copy in copies[:2]:
        copy.wait()
    row = lax.broadcasted_iota(jnp.int32, (PAD, tokens), 0)
    told = jnp.broadcast_to(docs[...].astype(F32), (PAD, tokens))
    for block in range(tokens // BLOCK):
        told = jnp.where(row == 1 + block, tenant[block].astype(F32), told)
    message[tokens:, :] = told.astype(BF16)
    for copy in copies[2:]:
        copy.wait()


def pack(block_tenant, keys, values, docs, heads_dev):
    tokens = keys.shape[0]
    return pl.pallas_call(
        functools.partial(pack_kernel, heads_dev),
        in_specs=[HBM] * 4,
        out_specs=VMEM,
        out_shape=jax.ShapeDtypeStruct((tokens + PAD, 2 * HD), BF16),
        scratch_shapes=[
            pltpu.SMEM(block_tenant.shape, jnp.int32),
            pltpu.VMEM((1, tokens), jnp.int32),
            pltpu.SemaphoreType.DMA((4,)),
        ],
        name="pack",
        compiler_params=pltpu.CompilerParams(vmem_limit_bytes=PACK_LIMIT),
        cost_estimate=pl.CostEstimate(flops=0, bytes_accessed=1 << 18, transcendentals=0),
    )(block_tenant, keys, values, docs.reshape(1, tokens))


def columns_kernel(owners, adapter_b, after, *refs):
    outs, sems = refs[:owners], refs[owners]
    width = outs[0].shape[1]
    adp = lax.axis_index("adp")
    copies = []
    for s in range(owners):
        start = pl.multiple_of(lax.rem(adp + s, owners) * width, 128)
        copies.append(pltpu.make_async_copy(adapter_b.at[0, :, pl.ds(start, width)], outs[s], sems.at[s]))
        copies[-1].start()
    for copy in copies:
        copy.wait()


def columns(adapter_b, after, owners):
    width = adapter_b.shape[2] // owners
    return pl.pallas_call(
        functools.partial(columns_kernel, owners),
        in_specs=[ANY, ANY],
        out_specs=[VMEM] * owners,
        out_shape=[jax.ShapeDtypeStruct((RANK, width), BF16)] * owners,
        scratch_shapes=[pltpu.SemaphoreType.DMA((owners,))],
        name="columns",
        compiler_params=pltpu.CompilerParams(vmem_limit_bytes=8 << 20),
        cost_estimate=pl.CostEstimate(flops=1 << 33, bytes_accessed=1 << 19, transcendentals=0),
    )(adapter_b, after)


def lanes(x, times):
    return jnp.concatenate([x] * times, axis=1)


def rows(x, times):
    return jnp.concatenate([x] * times, axis=0)


def attend_kernel(shifts, first, last, owners, *refs):
    refs = list(refs)
    take = lambda count: [refs.pop(0) for _ in range(count)]
    q_ref, g_ref, docs_ref = take(3)
    own, other = take(len(shifts)), take(len(shifts))
    if not first:
        top_in, by_key_in, by_grad_in = take(3)
    if last:
        (low_ref,) = take(1)
        b_refs = take(owners)
        dq_ref, rank_ref, mine_ref, partner_ref = take(4)
    top, by_key, by_grad, bias = take(4)
    if last:
        (chosen,) = take(1)
    tokens, width = q_ref.shape
    heads = width // HD
    group = min(GROUP, heads)
    ctx = lax.axis_index("ctx")
    z, core = ctx // CORES, lax.rem(ctx, CORES)
    doc_row = lambda ref: ref[tokens : tokens + PAD, :][:1].astype(F32)

    docs = doc_row(docs_ref)
    first_doc = jnp.min(docs)
    row = lax.broadcasted_iota(jnp.int32, (tokens, tokens), 0)
    lane = lax.broadcasted_iota(jnp.int32, (tokens, tokens), 1)
    doc_column = jnp.sum(jnp.where(row == lane, docs, 0.0), axis=1, keepdims=True)

    def stacked(ref, h):
        return jnp.concatenate(
            [ref[:, i * HD : (i + 1) * HD] for i in range(h, h + group)], axis=0
        )

    def step(index, shift, old):
        keys = jnp.concatenate([own[index][:tokens, :HD], other[index][:tokens, :HD]], axis=0)
        values = jnp.concatenate([own[index][:tokens, HD:], other[index][:tokens, HD:]], axis=0)
        extended = jnp.concatenate([keys, jnp.ones((2 * tokens, HD), BF16)], axis=1)
        own_seen = doc_row(own[index]) == doc_column
        other_doc = doc_row(other[index])
        if shift == 0:
            own_seen = own_seen & (lane <= row)
            other_doc = jnp.where(core == 1, other_doc, -1.0)
        other_seen = other_doc == doc_column
        bias[:, :tokens] = jnp.where(own_seen, 0.0, far_below)
        bias[:, tokens:] = jnp.where(other_seen, 0.0, far_below)
        for h in range(0, heads, group):
            part = slice(h * tokens, (h + group) * tokens)
            scores = lax.dot_general(
                stacked(q_ref, h), keys, (((1,), (1,)), ((), ())), preferred_element_type=F32
            ) + rows(bias[...], group)
            block_top = jnp.broadcast_to(
                jnp.max(scores, axis=1, keepdims=True), (group * tokens, 128)
            )
            new_top = block_top if shift == 0 else jnp.maximum(old[0][part, :], block_top)
            p = jnp.exp2((scores - lanes(new_top, 2 * tokens // 128)) * log2_scale)
            grads = lax.dot_general(
                stacked(g_ref, h), values, (((1,), (1,)), ((), ())), preferred_element_type=F32
            )
            key_sum = jnp.dot(p.astype(BF16), extended, preferred_element_type=F32)
            grad_sum = jnp.dot((p * grads).astype(BF16), extended, preferred_element_type=F32)
            if shift:
                decay = lanes(jnp.exp2((old[0][part, :] - new_top) * log2_scale), 2)
                key_sum = key_sum + old[1][part, :] * decay
                grad_sum = grad_sum + old[2][part, :] * decay
            top[part, :] = new_top
            by_key[part, :] = key_sum
            by_grad[part, :] = grad_sum

    for index, shift in enumerate(shifts):
        if shift == 0:
            step(index, shift, None)
            continue
        old = (top, by_key, by_grad)
        latest = jnp.max(jnp.maximum(doc_row(own[index]), doc_row(other[index])))
        needed = (z >= shift) & (latest == first_doc)
        if index == 0:
            old = (top_in, by_key_in, by_grad_in)

            @pl.when(jnp.logical_not(needed))
            def _():
                for kept, given in zip((top, by_key, by_grad), old):
                    kept[...] = given[...]

        pl.when(needed)(functools.partial(step, index, shift, old))

    if not last:
        return
    for h in range(heads):
        part = slice(h * tokens, (h + 1) * tokens)
        inverse = 1.0 / by_key[part, HD:]
        delta = by_grad[part, HD:] * inverse
        dq = (by_grad[part, :HD] - delta * by_key[part, :HD]) * (inverse * logit_scale)
        dq_ref[:, h * HD : (h + 1) * HD] = dq.astype(BF16)

    half = width // CORES
    adp = lax.axis_index("adp")
    told = docs_ref[tokens:, :HD].astype(F32)
    for block in range(tokens // BLOCK):
        block_rows = slice(block * BLOCK, (block + 1) * BLOCK)
        partial = adapter_scale_factor * jnp.dot(
            low_ref[:, block_rows], dq_ref[block_rows, :], preferred_element_type=F32
        )
        out_rows = slice(block * RANK, (block + 1) * RANK)
        mine_ref[out_rows, :] = jnp.where(core == 0, partial[:, :half], partial[:, half:])
        partner_ref[out_rows, :] = jnp.where(
            core == 0, partial[:, half:], partial[:, :half]
        ).astype(BF16)

        tenant = jnp.max(told[1 + block : 2 + block]).astype(jnp.int32)
        holder = lax.rem(adp - tenant + owners, owners)
        for s in range(owners):

            @pl.when(holder == s)
            def _(s=s):
                chosen[...] = b_refs[s][...]

        rank_ref[block_rows, :] = adapter_scale_factor * lax.dot_general(
            dq_ref[block_rows, :], chosen[...], (((1,), (1,)), ((), ())), preferred_element_type=F32
        )


def attend(shifts, queries, grad_out, message, own, other, state=None, low_rank=None, b_cols=()):
    tokens, width = queries.shape
    heads = width // HD
    blocks = tokens // BLOCK
    sums = [
        ((heads * tokens, 128), F32),
        ((heads * tokens, 2 * HD), F32),
        ((heads * tokens, 2 * HD), F32),
    ]
    inputs = [queries, grad_out, message, *own, *other]
    scratch = [pltpu.VMEM((tokens, 2 * tokens), F32)]
    if state is not None:
        inputs += state
    if low_rank is None:
        outs = sums
    else:
        inputs += [low_rank.T, *b_cols]
        scratch = [pltpu.VMEM(*each) for each in sums] + scratch
        scratch += [
            pltpu.VMEM((RANK, width), BF16),
        ]
        outs = [
            ((tokens, width), BF16),
            ((tokens, RANK), F32),
            ((blocks * RANK, width // CORES), F32),
            ((blocks * RANK, width // CORES), BF16),
        ]
    return pl.pallas_call(
        functools.partial(
            attend_kernel, shifts, state is None, low_rank is not None, len(b_cols)
        ),
        in_specs=[VMEM] * len(inputs),
        out_specs=[VMEM] * len(outs),
        out_shape=[jax.ShapeDtypeStruct(*each) for each in outs],
        scratch_shapes=scratch,
        compiler_params=pltpu.CompilerParams(vmem_limit_bytes=30 << 20),
        cost_estimate=pl.CostEstimate(
            flops=len(shifts) * 12 * tokens * tokens * width,
            bytes_accessed=4 << 20,
            transcendentals=0,
        ),
        name="attend_" + "_".join(map(str, shifts[:4])),
    )(*inputs)


def tenants_kernel(owners, mine_ref, other_ref, own_notes, other_notes, rank_ref, *outs):
    blocks = mine_ref.shape[0] // RANK
    width = mine_ref.shape[1]
    share = rank_ref.shape[0] // owners
    adp = lax.axis_index("adp")
    told = [ref[ref.shape[0] - PAD :, :HD].astype(F32) for ref in (own_notes, other_notes)]
    for s in range(owners):
        owner = lax.rem(adp + s, owners)
        total = jnp.zeros((RANK, width), F32)
        for block in range(blocks):
            part = slice(block * RANK, (block + 1) * RANK)
            for each, ref in zip(told, (mine_ref, other_ref)):
                chosen = lanes(each[1 + block : 2 + block] == owner.astype(F32), width // HD)
                total = total + jnp.where(chosen, ref[part, :].astype(F32), 0.0)
        outs[s][:RANK, :] = total.astype(BF16)
        outs[s][RANK:, :] = jnp.zeros((PAD, width), BF16)
        for part in range(share // PAD):
            start = pl.multiple_of(owner * share + part * PAD, PAD)
            outs[s][RANK:, part * HD : part * HD + RANK] = rank_ref[pl.ds(start, PAD), :].astype(BF16)


def by_tenant(mine, other, own_message, other_message, ranks, owners):
    width = mine.shape[1]
    return pl.pallas_call(
        functools.partial(tenants_kernel, owners),
        in_specs=[VMEM] * 5,
        out_specs=[VMEM] * owners,
        out_shape=[jax.ShapeDtypeStruct((RANK + PAD, width), BF16)] * owners,
        name="by_tenant",
        **small(1 << 20),
    )(mine, other, own_message, other_message, ranks)


def columns_owner_kernel(owners, *refs):
    pieces, outs = refs[:owners], refs[owners:]
    ctx, adp = lax.axis_index("ctx"), lax.axis_index("adp")
    z = ctx // CORES
    for s in range(owners):
        source = lax.rem(adp - z - s + 2 * owners, owners)
        for j in range(owners):

            @pl.when(source == j)
            def _(s=s, j=j):
                outs[s][...] = pieces[j][:RANK, :]


def by_columns_owner(pieces):
    owners = len(pieces)
    width = pieces[0].shape[1]
    return pl.pallas_call(
        functools.partial(columns_owner_kernel, owners),
        in_specs=[VMEM] * owners,
        out_specs=[VMEM] * owners,
        out_shape=[jax.ShapeDtypeStruct((RANK, width), BF16)] * owners,
        name="by_columns_owner",
        **small(1 << 20),
    )(*pieces)


def finish_kernel(owners, *refs):
    dq_ref, pieces = refs[0], refs[1 : owners + 1]
    dq_hbm, rank_out, sem = refs[owners + 1 :]
    copy = pltpu.make_async_copy(dq_ref, dq_hbm, sem)
    copy.start()
    for part in range(rank_out.shape[0] // PAD):
        rank_out[part * PAD : (part + 1) * PAD, :] = sum(
            piece[RANK:, part * HD : part * HD + RANK].astype(F32) for piece in pieces
        )
    copy.wait()


def finish(dq, pieces, share):
    owners = len(pieces)
    return pl.pallas_call(
        functools.partial(finish_kernel, owners),
        in_specs=[VMEM] * (1 + owners),
        out_specs=[ANY, VMEM],
        out_shape=[
            jax.ShapeDtypeStruct(dq.shape, BF16),
            jax.ShapeDtypeStruct((share, RANK), F32),
        ],
        scratch_shapes=[pltpu.SemaphoreType.DMA],
        name="finish",
        **small(1 << 20),
    )(dq, *pieces)


def on_device(queries, keys, values, grad_out, docs, block_tenant, low_rank, adapter_b):
    positions, owners = lax.axis_size("ctx"), lax.axis_size("adp")
    chips = positions // CORES
    tokens = queries.shape[0]
    heads_dev = queries.shape[1] // HD
    swap = [(c, c ^ 1) for c in range(positions)]
    up = lambda s: [(c, (c + CORES * s) % positions) for c in range(positions)]
    along = lambda s: [(a, (a + s) % owners) for a in range(owners)]

    message = pack(block_tenant, keys, values, docs, heads_dev)
    far = {s: lax.ppermute(message, "ctx", up(s)) for s in reversed(range(1, chips))}
    own = [message] + [far[s] for s in range(1, chips)]
    other = [lax.ppermute(message, "ctx", swap)]
    b_out = columns(adapter_b, other[0], owners)
    b_cols = [b_out[0]] + [lax.ppermute(b_out[s], "adp", along(s)) for s in range(1, owners)]
    state = attend((0,), queries, grad_out, message, own[:1], other[:1])
    own[-1], b_cols[1] = lax.optimization_barrier((own[-1], b_cols[1]))
    far_other = lax.ppermute(own[-1], "ctx", swap)
    near, state, b_cols = lax.optimization_barrier((own[1:-1], state, b_cols))
    near_other = [lax.ppermute(m, "ctx", swap) for m in near]
    state = attend((chips - 1,), queries, grad_out, message, own[-1:], [far_other], state)
    grad_queries, ranks, mine, partner = attend(
        tuple(range(1, chips - 1)),
        queries,
        grad_out,
        message,
        near,
        near_other,
        state,
        low_rank,
        b_cols,
    )
    other_part = lax.ppermute(partner, "ctx", swap)
    pieces = by_tenant(mine, other_part, message, other[0], ranks, owners)
    pieces = [pieces[0]] + [
        lax.ppermute(pieces[s], "adp", along(s)) for s in range(1, owners)
    ]
    grad_queries, grad_low_rank = finish(grad_queries, pieces, tokens // owners)
    pieces = by_columns_owner(pieces)
    pieces = [pieces[0]] + [lax.ppermute(pieces[s], "ctx", up(s)) for s in range(1, chips)]
    grad_adapter = sum(piece.astype(F32) for piece in pieces)[None]
    return grad_queries, grad_low_rank, grad_adapter


def solution(mesh):
    placed = (
        P("ctx", "adp"),
        P("ctx", None),
        P("ctx", None),
        P("ctx", "adp"),
        P("ctx"),
        P("ctx"),
        P("ctx", None),
        P("adp", None, None),
    )
    return jax.shard_map(
        on_device,
        mesh=mesh,
        in_specs=placed,
        out_specs=(P("ctx", "adp"), P(("ctx", "adp"), None), P("adp", None, "ctx")),
        check_vma=False,
    )
```

```python
import functools

import jax
import jax.numpy as jnp
from jax import lax
from jax.experimental import pallas as pl
from jax.experimental.pallas import tpu as pltpu
from jax.sharding import PartitionSpec as P

QH = 32
KVH = 4
HD = 128
RANK = 64
BLOCK = 128
CORES = 2
PAD = 16
PACK_LIMIT = (64 << 20) - (1 << 18)

adapter_scale_factor = 2.0
far_below = -1e30
logit_scale = HD ** (-0.5)
log2_scale = logit_scale * 1.4426950408889634

VMEM = pl.BlockSpec(memory_space=pltpu.VMEM)
SMEM = pl.BlockSpec(memory_space=pltpu.SMEM)
ANY = pl.BlockSpec(memory_space=pl.ANY)
HBM = pl.BlockSpec(memory_space=pltpu.HBM)
BF16 = jnp.bfloat16
F32 = jnp.float32


def small(bytes_accessed):
    return dict(
        compiler_params=pltpu.CompilerParams(vmem_limit_bytes=8 << 20),
        cost_estimate=pl.CostEstimate(flops=0, bytes_accessed=bytes_accessed, transcendentals=0),
    )


def pack_kernel(heads_dev, tenant_hbm, keys, values, docs_hbm, message, tenant, docs, sems):
    tokens = keys.shape[0]
    kv = lax.axis_index("adp") * heads_dev // (QH // KVH)
    head = pl.ds(pl.multiple_of(kv * HD, HD), HD)
    copies = [
        pltpu.make_async_copy(docs_hbm, docs, sems.at[0]),
        pltpu.make_async_copy(tenant_hbm, tenant, sems.at[1]),
        pltpu.make_async_copy(keys.at[:, head], message.at[pl.ds(0, tokens), pl.ds(0, HD)], sems.at[2]),
        pltpu.make_async_copy(values.at[:, head], message.at[pl.ds(0, tokens), pl.ds(HD, HD)], sems.at[3]),
    ]
    for copy in copies:
        copy.start()
    for copy in copies[:2]:
        copy.wait()
    row = lax.broadcasted_iota(jnp.int32, (PAD, tokens), 0)
    told = jnp.broadcast_to(docs[...].astype(F32), (PAD, tokens))
    for block in range(tokens // BLOCK):
        told = jnp.where(row == 1 + block, tenant[block].astype(F32), told)
    message[tokens:, :] = told.astype(BF16)
    for copy in copies[2:]:
        copy.wait()


def pack(block_tenant, keys, values, docs, heads_dev):
    tokens = keys.shape[0]
    return pl.pallas_call(
        functools.partial(pack_kernel, heads_dev),
        in_specs=[HBM] * 4,
        out_specs=VMEM,
        out_shape=jax.ShapeDtypeStruct((tokens + PAD, 2 * HD), BF16),
        scratch_shapes=[
            pltpu.SMEM(block_tenant.shape, jnp.int32),
            pltpu.VMEM((1, tokens), jnp.int32),
            pltpu.SemaphoreType.DMA((4,)),
        ],
        name="pack",
        compiler_params=pltpu.CompilerParams(vmem_limit_bytes=PACK_LIMIT),
        cost_estimate=pl.CostEstimate(flops=0, bytes_accessed=1 << 18, transcendentals=0),
    )(block_tenant, keys, values, docs.reshape(1, tokens))


def columns_kernel(owners, adapter_b, after, *refs):
    outs, sems = refs[:-1], refs[-1]
    width = outs[0].shape[1]
    adp = lax.axis_index("adp")
    core = lax.rem(lax.axis_index("ctx"), CORES)
    copies = []
    for s, out in enumerate(outs):
        owner = lax.rem(adp + jnp.where(core == 0, s, owners - s), owners)
        start = pl.multiple_of(owner * width, 128)
        copies.append(pltpu.make_async_copy(adapter_b.at[0, :, pl.ds(start, width)], out, sems.at[s]))
        copies[-1].start()
    for copy in copies:
        copy.wait()


def columns(adapter_b, after, owners):
    width = adapter_b.shape[2] // owners
    count = owners // 2 + 1
    return pl.pallas_call(
        functools.partial(columns_kernel, owners),
        in_specs=[ANY, ANY],
        out_specs=[VMEM] * count,
        out_shape=[jax.ShapeDtypeStruct((RANK, width), BF16)] * count,
        scratch_shapes=[pltpu.SemaphoreType.DMA((count,))],
        name="columns",
        compiler_params=pltpu.CompilerParams(vmem_limit_bytes=8 << 20),
        cost_estimate=pl.CostEstimate(flops=1 << 33, bytes_accessed=1 << 19, transcendentals=0),
    )(adapter_b, after)


def lanes(x, times):
    return jnp.concatenate([x] * times, axis=1)


def rows(parts):
    return jnp.concatenate(parts, axis=0)


def attend_kernel(shifts, parts, first, last, owners, *refs):
    refs = list(refs)
    take = lambda count: [refs.pop(0) for _ in range(count)]
    q_ref, g_ref, docs_ref = take(3)
    own, other = take(len(shifts)), take(len(shifts))
    if not first:
        given = take(3)
    if last:
        (low_ref,) = take(1)
        b_refs = take(owners)
        dq_refs = take(parts[0])
        dq_ref, partial_ref = take(2)
        rank_refs = take(parts[0])
    sums = take(3)
    (bias,) = take(1)
    tokens, width = q_ref.shape
    half = width // CORES
    group = half // HD
    part_rows = group * tokens
    ctx = lax.axis_index("ctx")
    z, core = ctx // CORES, lax.rem(ctx, CORES)
    offset = lambda part: pl.multiple_of((core if part else 1 - core) * half, HD)
    doc_row = lambda ref: ref[tokens : tokens + PAD, :][:1].astype(F32)

    docs = doc_row(docs_ref)
    first_doc = jnp.min(docs)
    row = lax.broadcasted_iota(jnp.int32, (tokens, tokens), 0)
    lane = lax.broadcasted_iota(jnp.int32, (tokens, tokens), 1)
    doc_column = jnp.sum(jnp.where(row == lane, docs, 0.0), axis=1, keepdims=True)

    def stacked(ref, part):
        return rows([ref[:, pl.ds(offset(part) + i * HD, HD)] for i in range(group)])

    def place(ref, part):
        start = 0 if ref.shape[0] == part_rows else part * part_rows
        return slice(start, start + part_rows)

    def step(indices, old):
        messages = [ref for i in indices for ref in (own[i], other[i])]
        keys = rows([ref[:tokens, :HD] for ref in messages])
        values = rows([ref[:tokens, HD:] for ref in messages])
        count = len(messages) * tokens
        extended = jnp.concatenate([keys, jnp.ones((count, HD), BF16)], axis=1)
        for i, ref in enumerate(messages):
            key_docs = doc_row(ref)
            if old is None and i == 1:
                key_docs = jnp.where(core == 1, key_docs, -1.0)
            seen = key_docs == doc_column
            if old is None and i == 0:
                seen = seen & (lane <= row)
            bias[:, i * tokens : (i + 1) * tokens] = jnp.where(seen, 0.0, far_below)
        for part in parts:
            scores = lax.dot_general(
                stacked(q_ref, part), keys, (((1,), (1,)), ((), ())), preferred_element_type=F32
            ) + rows([bias[:, :count]] * group)
            new_top = jnp.broadcast_to(jnp.max(scores, axis=1, keepdims=True), (part_rows, 128))
            if old is not None:
                old_top = old[0][place(old[0], part), :]
                new_top = jnp.maximum(old_top, new_top)
            p = jnp.exp2((scores - lanes(new_top, count // 128)) * log2_scale)
            grads = lax.dot_general(
                stacked(g_ref, part), values, (((1,), (1,)), ((), ())), preferred_element_type=F32
            )
            by_key = jnp.dot(p.astype(BF16), extended, preferred_element_type=F32)
            by_grad = jnp.dot((p * grads).astype(BF16), extended, preferred_element_type=F32)
            if old is not None:
                decay = lanes(jnp.exp2((old_top - new_top) * log2_scale), 2)
                by_key = by_key + old[1][place(old[1], part), :] * decay
                by_grad = by_grad + old[2][place(old[2], part), :] * decay
            for ref, value in zip(sums, (new_top, by_key, by_grad)):
                ref[place(ref, part), :] = value

    if first:
        step([0], None)
    else:
        needed = []
        for index, shift in enumerate(shifts):
            latest = jnp.max(jnp.maximum(doc_row(own[index]), doc_row(other[index])))
            needed.append((z >= shift) & (latest == first_doc))
        for index in range(len(shifts)):
            old = sums if index else given
            pl.when(needed[index])(functools.partial(step, [index], old))
            if index == 0:

                @pl.when(jnp.logical_not(needed[0]))
                def _():
                    for part in parts:
                        for kept, ref in zip(sums, given):
                            kept[place(kept, part), :] = ref[place(ref, part), :]

    if not last:
        return
    _, by_key, by_grad = sums
    (part,) = parts
    for h in range(group):
        head_rows = slice(h * tokens, (h + 1) * tokens)
        inverse = 1.0 / by_key[head_rows, HD:]
        delta = by_grad[head_rows, HD:] * inverse
        dq = (by_grad[head_rows, :HD] - delta * by_key[head_rows, :HD]) * (inverse * logit_scale)
        dq_ref[:, h * HD : (h + 1) * HD] = dq.astype(BF16)

    adp = lax.axis_index("adp")
    told = docs_ref[tokens:, :HD].astype(F32)
    for block in range(tokens // BLOCK):
        block_rows = slice(block * BLOCK, (block + 1) * BLOCK)
        partial = adapter_scale_factor * jnp.dot(
            low_ref[:, block_rows], dq_ref[block_rows, :], preferred_element_type=F32
        )
        partial_ref[block * RANK : (block + 1) * RANK, :] = partial.astype(partial_ref.dtype)

        if part == 0:
            continue
        tenant = jnp.max(told[1 + block : 2 + block]).astype(jnp.int32)
        back = lax.rem(adp - tenant + owners, owners)
        holder = jnp.where(core == 0, back, lax.rem(owners - back, owners))
        for s in range(owners):

            @pl.when(holder == s)
            def _(s=s, block_rows=block_rows):
                rank_refs[0][block_rows, :] = adapter_scale_factor * sum(
                    lax.dot_general(
                        dq[block_rows, :],
                        b_refs[s][:, pl.ds(offset(each), half)],
                        (((1,), (1,)), ((), ())),
                        preferred_element_type=F32,
                    )
                    for each, dq in enumerate([*dq_refs, dq_ref])
                )


def attend(shifts, queries, grad_out, message, own, other, state=(), final=None):
    tokens, width = queries.shape
    half = width // CORES
    blocks = tokens // BLOCK
    parts = (0, 1) if final is None else (final[0],)
    stack = len(parts) * half // HD * tokens
    sums = [((stack, 128), F32), ((stack, 2 * HD), F32), ((stack, 2 * HD), F32)]
    inputs = [queries, grad_out, message, *own, *other, *state]
    scratch = [pltpu.VMEM((tokens, 2 * tokens), F32)]
    owners = 0
    if final is None:
        outs = sums
    else:
        part, low_rank, *rest = final
        b_cols = rest[1] if part else ()
        owners = len(b_cols)
        inputs += [low_rank.T, *b_cols, *rest[:1]]
        scratch = [pltpu.VMEM(*each) for each in sums] + scratch
        outs = [
            ((tokens, half), BF16),
            ((blocks * RANK, half), F32 if part else BF16),
        ]
        outs += [((tokens, RANK), F32)] * part
    return pl.pallas_call(
        functools.partial(attend_kernel, shifts, parts, not state, final is not None, owners),
        in_specs=[VMEM] * len(inputs),
        out_specs=[VMEM] * len(outs),
        out_shape=[jax.ShapeDtypeStruct(*each) for each in outs],
        scratch_shapes=scratch,
        compiler_params=pltpu.CompilerParams(vmem_limit_bytes=30 << 20),
        cost_estimate=pl.CostEstimate(
            flops=len(shifts) * 6 * len(parts) * tokens * tokens * width,
            bytes_accessed=4 << 20,
            transcendentals=0,
        ),
        name="attend_" + "_".join(map(str, shifts[:4])) + ("" if final is None else f"_part{part}"),
    )(*inputs)


def tenants_kernel(owners, mine_ref, other_ref, own_notes, other_notes, rank_ref, *outs):
    blocks = mine_ref.shape[0] // RANK
    width = mine_ref.shape[1]
    share = rank_ref.shape[0] // owners
    adp = lax.axis_index("adp")
    told = [ref[ref.shape[0] - PAD :, :HD].astype(F32) for ref in (own_notes, other_notes)]
    for s in range(owners):
        owner = lax.rem(adp + s, owners)
        total = jnp.zeros((RANK, width), F32)
        for block in range(blocks):
            part = slice(block * RANK, (block + 1) * RANK)
            for each, ref in zip(told, (mine_ref, other_ref)):
                chosen = lanes(each[1 + block : 2 + block] == owner.astype(F32), width // HD)
                total = total + jnp.where(chosen, ref[part, :].astype(F32), 0.0)
        outs[s][:RANK, :] = total.astype(BF16)
        outs[s][RANK:, :] = jnp.zeros((PAD, width), BF16)
        for part in range(share // PAD):
            start = pl.multiple_of(owner * share + part * PAD, PAD)
            outs[s][RANK:, part * HD : part * HD + RANK] = rank_ref[pl.ds(start, PAD), :].astype(BF16)


def by_tenant(mine, other, own_message, other_message, ranks, owners):
    width = mine.shape[1]
    return pl.pallas_call(
        functools.partial(tenants_kernel, owners),
        in_specs=[VMEM] * 5,
        out_specs=[VMEM] * owners,
        out_shape=[jax.ShapeDtypeStruct((RANK + PAD, width), BF16)] * owners,
        name="by_tenant",
        **small(1 << 20),
    )(mine, other, own_message, other_message, ranks)


def columns_owner_kernel(owners, *refs):
    pieces, outs = refs[:owners], refs[owners:]
    ctx, adp = lax.axis_index("ctx"), lax.axis_index("adp")
    z = ctx // CORES
    for s in range(owners):
        source = lax.rem(adp - z - s + 2 * owners, owners)
        for j in range(owners):

            @pl.when(source == j)
            def _(s=s, j=j):
                outs[s][...] = pieces[j][:RANK, :]


def by_columns_owner(pieces):
    owners = len(pieces)
    width = pieces[0].shape[1]
    return pl.pallas_call(
        functools.partial(columns_owner_kernel, owners),
        in_specs=[VMEM] * owners,
        out_specs=[VMEM] * owners,
        out_shape=[jax.ShapeDtypeStruct((RANK, width), BF16)] * owners,
        name="by_columns_owner",
        **small(1 << 20),
    )(*pieces)


def finish_kernel(owners, *refs):
    parts, pieces = refs[:CORES], refs[CORES : owners + CORES]
    dq_hbm, rank_out, sem = refs[owners + CORES :]
    half = parts[0].shape[1]
    core = lax.rem(lax.axis_index("ctx"), CORES)
    copies = []
    for part, ref in enumerate(parts):
        start = pl.multiple_of((core if part else 1 - core) * half, HD)
        copies.append(pltpu.make_async_copy(ref, dq_hbm.at[:, pl.ds(start, half)], sem.at[part]))
        copies[-1].start()
    for part in range(rank_out.shape[0] // PAD):
        rank_out[part * PAD : (part + 1) * PAD, :] = sum(
            piece[RANK:, part * HD : part * HD + RANK].astype(F32) for piece in pieces
        )
    for copy in copies:
        copy.wait()


def finish(dq, pieces, share):
    owners = len(pieces)
    return pl.pallas_call(
        functools.partial(finish_kernel, owners),
        in_specs=[VMEM] * (CORES + owners),
        out_specs=[ANY, VMEM],
        out_shape=[
            jax.ShapeDtypeStruct((dq[0].shape[0], CORES * dq[0].shape[1]), BF16),
            jax.ShapeDtypeStruct((share, RANK), F32),
        ],
        scratch_shapes=[pltpu.SemaphoreType.DMA((CORES,))],
        name="finish",
        **small(1 << 20),
    )(*dq, *pieces)


def on_device(queries, keys, values, grad_out, docs, block_tenant, low_rank, adapter_b):
    positions, owners = lax.axis_size("ctx"), lax.axis_size("adp")
    chips = positions // CORES
    tokens = queries.shape[0]
    heads_dev = queries.shape[1] // HD
    swap = [(c, c ^ 1) for c in range(positions)]
    up = lambda s: [(c, (c + CORES * s) % positions) for c in range(positions)]
    along = lambda s: [(a, (a + s) % owners) for a in range(owners)]

    message = pack(block_tenant, keys, values, docs, heads_dev)
    shifts = [2, *range(3, chips), 1]
    arrive = {s: lax.ppermute(message, "ctx", up(s)) for s in (2, 1, *range(3, chips))}
    own = [arrive[s] for s in shifts]
    mine_other = lax.ppermute(message, "ctx", swap)
    b_out = columns(adapter_b, mine_other, owners)

    def apart(s):
        return [
            (c * owners + a, c * owners + (a + (s if c % CORES == 0 else -s)) % owners)
            for c in range(positions)
            for a in range(owners)
        ]

    b_in = [lax.ppermute(b_out[s], ("ctx", "adp"), apart(s)) for s in range(1, owners // 2 + 1)]
    heads = (queries, grad_out, message)
    state = attend((0,), *heads, [message], [mine_other])
    own = [*own[1:], own[0]]
    own, state, b_in = lax.optimization_barrier((own, state, b_in))
    other = [lax.ppermute(m, "ctx", swap) for m in own]
    b_swapped = [lax.ppermute(x, "ctx", swap) for x in b_in[:-1]]
    b_cols = [b_out[0], *b_in, *reversed(b_swapped)]
    own, other = [[each[-2], each[-1], *each[:-2]] for each in (own, other)]
    last = functools.partial(attend, tuple(range(1, chips)), *heads, own, other, state)
    dq_other, partner = last((0, low_rank))
    other_part = lax.ppermute(partner, "ctx", swap)
    dq_mine, mine, ranks = last((1, low_rank, dq_other, b_cols))
    pieces = by_tenant(mine, other_part, message, mine_other, ranks, owners)
    pieces = [pieces[0]] + [
        lax.ppermute(pieces[s], "adp", along(s)) for s in range(1, owners)
    ]
    grad_queries, grad_low_rank = finish([dq_other, dq_mine], pieces, tokens // owners)
    pieces = by_columns_owner(pieces)
    pieces = [pieces[0]] + [lax.ppermute(pieces[s], "ctx", up(s)) for s in range(1, chips)]
    grad_adapter = sum(piece.astype(F32) for piece in pieces)[None]
    return grad_queries, grad_low_rank, grad_adapter


def solution(mesh):
    placed = (
        P("ctx", "adp"),
        P("ctx", None),
        P("ctx", None),
        P("ctx", "adp"),
        P("ctx"),
        P("ctx"),
        P("ctx", None),
        P("adp", None, None),
    )
    return jax.shard_map(
        on_device,
        mesh=mesh,
        in_specs=placed,
        out_specs=(P("ctx", "adp"), P(("ctx", "adp"), None), P("adp", None, "ctx")),
        check_vma=False,
    )
```

```python
import functools

import jax
import jax.numpy as jnp
from jax import lax
from jax.experimental import pallas as pl
from jax.experimental.pallas import tpu as pltpu
from jax.sharding import PartitionSpec as P

QH = 32
KVH = 4
HD = 128
RANK = 64
BLOCK = 128
CORES = 2
PAD = 16
PACK_LIMIT = (64 << 20) - (1 << 18)

adapter_scale_factor = 2.0
far_below = -1e30
logit_scale = HD ** (-0.5)
log2_scale = logit_scale * 1.4426950408889634

VMEM = pl.BlockSpec(memory_space=pltpu.VMEM)
SMEM = pl.BlockSpec(memory_space=pltpu.SMEM)
ANY = pl.BlockSpec(memory_space=pl.ANY)
HBM = pl.BlockSpec(memory_space=pltpu.HBM)
BF16 = jnp.bfloat16
F32 = jnp.float32


def small(bytes_accessed):
    return dict(
        compiler_params=pltpu.CompilerParams(vmem_limit_bytes=8 << 20),
        cost_estimate=pl.CostEstimate(flops=0, bytes_accessed=bytes_accessed, transcendentals=0),
    )


def pack_kernel(heads_dev, tenant_hbm, keys, values, docs_hbm, message, tenant, docs, sems):
    tokens = keys.shape[0]
    kv = lax.axis_index("adp") * heads_dev // (QH // KVH)
    head = pl.ds(pl.multiple_of(kv * HD, HD), HD)
    copies = [
        pltpu.make_async_copy(docs_hbm, docs, sems.at[0]),
        pltpu.make_async_copy(tenant_hbm, tenant, sems.at[1]),
        pltpu.make_async_copy(keys.at[:, head], message.at[pl.ds(0, tokens), pl.ds(0, HD)], sems.at[2]),
        pltpu.make_async_copy(values.at[:, head], message.at[pl.ds(0, tokens), pl.ds(HD, HD)], sems.at[3]),
    ]
    for copy in copies:
        copy.start()
    for copy in copies[:2]:
        copy.wait()
    row = lax.broadcasted_iota(jnp.int32, (PAD, tokens), 0)
    told = jnp.broadcast_to(docs[...].astype(F32), (PAD, tokens))
    for block in range(tokens // BLOCK):
        told = jnp.where(row == 1 + block, tenant[block].astype(F32), told)
    message[tokens:, :] = told.astype(BF16)
    for copy in copies[2:]:
        copy.wait()


def pack(block_tenant, keys, values, docs, heads_dev):
    tokens = keys.shape[0]
    return pl.pallas_call(
        functools.partial(pack_kernel, heads_dev),
        in_specs=[HBM] * 4,
        out_specs=VMEM,
        out_shape=jax.ShapeDtypeStruct((tokens + PAD, 2 * HD), BF16),
        scratch_shapes=[
            pltpu.SMEM(block_tenant.shape, jnp.int32),
            pltpu.VMEM((1, tokens), jnp.int32),
            pltpu.SemaphoreType.DMA((4,)),
        ],
        name="pack",
        compiler_params=pltpu.CompilerParams(vmem_limit_bytes=PACK_LIMIT),
        cost_estimate=pl.CostEstimate(flops=0, bytes_accessed=1 << 18, transcendentals=0),
    )(block_tenant, keys, values, docs.reshape(1, tokens))


def columns_kernel(owners, adapter_b, after, *refs):
    outs, sems = refs[:-1], refs[-1]
    width = outs[0].shape[1]
    adp = lax.axis_index("adp")
    core = lax.rem(lax.axis_index("ctx"), CORES)
    copies = []
    for s, out in enumerate(outs):
        owner = lax.rem(adp + jnp.where(core == 0, s, owners - s), owners)
        start = pl.multiple_of(owner * width, 128)
        copies.append(pltpu.make_async_copy(adapter_b.at[0, :, pl.ds(start, width)], out, sems.at[s]))
        copies[-1].start()
    for copy in copies:
        copy.wait()


def columns(adapter_b, after, owners):
    width = adapter_b.shape[2] // owners
    count = owners // 2 + 1
    return pl.pallas_call(
        functools.partial(columns_kernel, owners),
        in_specs=[ANY, ANY],
        out_specs=[VMEM] * count,
        out_shape=[jax.ShapeDtypeStruct((RANK, width), BF16)] * count,
        scratch_shapes=[pltpu.SemaphoreType.DMA((count,))],
        name="columns",
        compiler_params=pltpu.CompilerParams(vmem_limit_bytes=8 << 20),
        cost_estimate=pl.CostEstimate(flops=1 << 33, bytes_accessed=1 << 19, transcendentals=0),
    )(adapter_b, after)


def lanes(x, times):
    return jnp.concatenate([x] * times, axis=1)


def rows(parts):
    return jnp.concatenate(parts, axis=0)


def attend_kernel(shifts, parts, first, last, owners, *refs):
    refs = list(refs)
    take = lambda count: [refs.pop(0) for _ in range(count)]
    q_ref, g_ref, docs_ref = take(3)
    own, other = take(len(shifts)), take(len(shifts))
    if not first:
        given = take(3)
    if last:
        (low_ref,) = take(1)
        b_refs = take(owners)
        dq_refs = take(parts[0])
        dq_ref, partial_ref = take(2)
        rank_refs = take(parts[0])
    sums = take(3)
    (bias,) = take(1)
    tokens, width = q_ref.shape
    half = width // CORES
    group = half // HD
    part_rows = group * tokens
    ctx = lax.axis_index("ctx")
    z, core = ctx // CORES, lax.rem(ctx, CORES)
    offset = lambda part: pl.multiple_of((core if part else 1 - core) * half, HD)
    doc_row = lambda ref: ref[tokens : tokens + PAD, :][:1].astype(F32)

    docs = doc_row(docs_ref)
    first_doc = jnp.min(docs)
    row = lax.broadcasted_iota(jnp.int32, (tokens, tokens), 0)
    lane = lax.broadcasted_iota(jnp.int32, (tokens, tokens), 1)
    doc_column = jnp.sum(jnp.where(row == lane, docs, 0.0), axis=1, keepdims=True)

    def stacked(ref, part):
        return rows([ref[:, pl.ds(offset(part) + i * HD, HD)] for i in range(group)])

    def place(ref, part):
        start = 0 if ref.shape[0] == part_rows else part * part_rows
        return slice(start, start + part_rows)

    def step(indices, old, later_core=False):
        messages = [ref for i in indices for ref in (own[i], other[i])]
        if later_core:
            (i,) = indices
            messages = [jnp.where(core == 1, own[i][...], other[i][...])]
        keys = rows([ref[:tokens, :HD] for ref in messages])
        values = rows([ref[:tokens, HD:] for ref in messages])
        count = len(messages) * tokens
        extended = jnp.concatenate([keys, jnp.ones((count, HD), BF16)], axis=1)
        for i, ref in enumerate(messages):
            key_docs = doc_row(ref)
            if old is None and i == 1:
                key_docs = jnp.where(core == 1, key_docs, -1.0)
            seen = key_docs == doc_column
            if old is None and i == 0:
                seen = seen & (lane <= row)
            bias[:, i * tokens : (i + 1) * tokens] = jnp.where(seen, 0.0, far_below)
        for part in parts:
            scores = lax.dot_general(
                stacked(q_ref, part), keys, (((1,), (1,)), ((), ())), preferred_element_type=F32
            ) + rows([bias[:, :count]] * group)
            new_top = jnp.broadcast_to(jnp.max(scores, axis=1, keepdims=True), (part_rows, 128))
            if old is not None:
                old_top = old[0][place(old[0], part), :]
                new_top = jnp.maximum(old_top, new_top)
            p = jnp.exp2((scores - lanes(new_top, count // 128)) * log2_scale)
            grads = lax.dot_general(
                stacked(g_ref, part), values, (((1,), (1,)), ((), ())), preferred_element_type=F32
            )
            by_key = jnp.dot(p.astype(BF16), extended, preferred_element_type=F32)
            by_grad = jnp.dot((p * grads).astype(BF16), extended, preferred_element_type=F32)
            if old is not None:
                decay = lanes(jnp.exp2((old_top - new_top) * log2_scale), 2)
                by_key = by_key + old[1][place(old[1], part), :] * decay
                by_grad = by_grad + old[2][place(old[2], part), :] * decay
            for ref, value in zip(sums, (new_top, by_key, by_grad)):
                ref[place(ref, part), :] = value

    if first:
        step([0], None)
    else:
        needed, both = [], []
        for index, shift in enumerate(shifts):
            doc_rows = doc_row(own[index]), doc_row(other[index])
            latest = jnp.max(jnp.maximum(*doc_rows))
            needed.append((z >= shift) & (latest == first_doc))
            both.append(jnp.max(jnp.where(core == 0, *doc_rows)) == first_doc)
        for index in range(len(shifts)):
            old = sums if index else given
            pl.when(needed[index] & both[index])(functools.partial(step, [index], old))
            pl.when(needed[index] & jnp.logical_not(both[index]))(
                functools.partial(step, [index], old, True)
            )
            if index == 0:

                @pl.when(jnp.logical_not(needed[0]))
                def _():
                    for part in parts:
                        for kept, ref in zip(sums, given):
                            kept[place(kept, part), :] = ref[place(ref, part), :]

    if not last:
        return
    _, by_key, by_grad = sums
    (part,) = parts
    for h in range(group):
        head_rows = slice(h * tokens, (h + 1) * tokens)
        inverse = 1.0 / by_key[head_rows, HD:]
        delta = by_grad[head_rows, HD:] * inverse
        dq = (by_grad[head_rows, :HD] - delta * by_key[head_rows, :HD]) * (inverse * logit_scale)
        dq_ref[:, h * HD : (h + 1) * HD] = dq.astype(BF16)

    adp = lax.axis_index("adp")
    told = docs_ref[tokens:, :HD].astype(F32)
    for block in range(tokens // BLOCK):
        block_rows = slice(block * BLOCK, (block + 1) * BLOCK)
        partial = adapter_scale_factor * jnp.dot(
            low_ref[:, block_rows], dq_ref[block_rows, :], preferred_element_type=F32
        )
        partial_ref[block * RANK : (block + 1) * RANK, :] = partial.astype(partial_ref.dtype)

        if part == 0:
            continue
        tenant = jnp.max(told[1 + block : 2 + block]).astype(jnp.int32)
        back = lax.rem(adp - tenant + owners, owners)
        holder = jnp.where(core == 0, back, lax.rem(owners - back, owners))
        for s in range(owners):

            @pl.when(holder == s)
            def _(s=s, block_rows=block_rows):
                rank_refs[0][block_rows, :] = adapter_scale_factor * sum(
                    lax.dot_general(
                        dq[block_rows, :],
                        b_refs[s][:, pl.ds(offset(each), half)],
                        (((1,), (1,)), ((), ())),
                        preferred_element_type=F32,
                    )
                    for each, dq in enumerate([*dq_refs, dq_ref])
                )


def attend(shifts, queries, grad_out, message, own, other, state=(), final=None):
    tokens, width = queries.shape
    half = width // CORES
    blocks = tokens // BLOCK
    parts = (0, 1) if final is None else (final[0],)
    stack = len(parts) * half // HD * tokens
    sums = [((stack, 128), F32), ((stack, 2 * HD), F32), ((stack, 2 * HD), F32)]
    inputs = [queries, grad_out, message, *own, *other, *state]
    scratch = [pltpu.VMEM((tokens, 2 * tokens), F32)]
    owners = 0
    if final is None:
        outs = sums
    else:
        part, low_rank, *rest = final
        b_cols = rest[1] if part else ()
        owners = len(b_cols)
        inputs += [low_rank.T, *b_cols, *rest[:1]]
        scratch = [pltpu.VMEM(*each) for each in sums] + scratch
        outs = [
            ((tokens, half), BF16),
            ((blocks * RANK, half), F32 if part else BF16),
        ]
        outs += [((tokens, RANK), F32)] * part
    return pl.pallas_call(
        functools.partial(attend_kernel, shifts, parts, not state, final is not None, owners),
        in_specs=[VMEM] * len(inputs),
        out_specs=[VMEM] * len(outs),
        out_shape=[jax.ShapeDtypeStruct(*each) for each in outs],
        scratch_shapes=scratch,
        compiler_params=pltpu.CompilerParams(vmem_limit_bytes=30 << 20),
        cost_estimate=pl.CostEstimate(
            flops=len(shifts) * 6 * len(parts) * tokens * tokens * width,
            bytes_accessed=4 << 20,
            transcendentals=0,
        ),
        name="attend_" + "_".join(map(str, shifts[:4])) + ("" if final is None else f"_part{part}"),
    )(*inputs)


def tenants_kernel(owners, mine_ref, other_ref, own_notes, other_notes, rank_ref, *outs):
    blocks = mine_ref.shape[0] // RANK
    width = mine_ref.shape[1]
    share = rank_ref.shape[0] // owners
    adp = lax.axis_index("adp")
    told = [ref[ref.shape[0] - PAD :, :HD].astype(F32) for ref in (own_notes, other_notes)]
    for s in range(owners):
        owner = lax.rem(adp + s, owners)
        total = jnp.zeros((RANK, width), F32)
        for block in range(blocks):
            part = slice(block * RANK, (block + 1) * RANK)
            for each, ref in zip(told, (mine_ref, other_ref)):
                chosen = lanes(each[1 + block : 2 + block] == owner.astype(F32), width // HD)
                total = total + jnp.where(chosen, ref[part, :].astype(F32), 0.0)
        outs[s][:RANK, :] = total.astype(BF16)
        outs[s][RANK:, :] = jnp.zeros((PAD, width), BF16)
        for part in range(share // PAD):
            start = pl.multiple_of(owner * share + part * PAD, PAD)
            outs[s][RANK:, part * HD : part * HD + RANK] = rank_ref[pl.ds(start, PAD), :].astype(BF16)


def by_tenant(mine, other, own_message, other_message, ranks, owners):
    width = mine.shape[1]
    return pl.pallas_call(
        functools.partial(tenants_kernel, owners),
        in_specs=[VMEM] * 5,
        out_specs=[VMEM] * owners,
        out_shape=[jax.ShapeDtypeStruct((RANK + PAD, width), BF16)] * owners,
        name="by_tenant",
        **small(1 << 20),
    )(mine, other, own_message, other_message, ranks)


def columns_owner_kernel(owners, *refs):
    pieces, outs = refs[:owners], refs[owners:]
    ctx, adp = lax.axis_index("ctx"), lax.axis_index("adp")
    z = ctx // CORES
    for s in range(owners):
        source = lax.rem(adp - z - s + 2 * owners, owners)
        for j in range(owners):

            @pl.when(source == j)
            def _(s=s, j=j):
                outs[s][...] = pieces[j][:RANK, :]


def by_columns_owner(pieces):
    owners = len(pieces)
    width = pieces[0].shape[1]
    return pl.pallas_call(
        functools.partial(columns_owner_kernel, owners),
        in_specs=[VMEM] * owners,
        out_specs=[VMEM] * owners,
        out_shape=[jax.ShapeDtypeStruct((RANK, width), BF16)] * owners,
        name="by_columns_owner",
        **small(1 << 20),
    )(*pieces)


def finish_kernel(owners, *refs):
    parts, pieces = refs[:CORES], refs[CORES : owners + CORES]
    dq_hbm, rank_out, sem = refs[owners + CORES :]
    half = parts[0].shape[1]
    core = lax.rem(lax.axis_index("ctx"), CORES)
    copies = []
    for part, ref in enumerate(parts):
        start = pl.multiple_of((core if part else 1 - core) * half, HD)
        copies.append(pltpu.make_async_copy(ref, dq_hbm.at[:, pl.ds(start, half)], sem.at[part]))
        copies[-1].start()
    for part in range(rank_out.shape[0] // PAD):
        rank_out[part * PAD : (part + 1) * PAD, :] = sum(
            piece[RANK:, part * HD : part * HD + RANK].astype(F32) for piece in pieces
        )
    for copy in copies:
        copy.wait()


def finish(dq, pieces, share):
    owners = len(pieces)
    return pl.pallas_call(
        functools.partial(finish_kernel, owners),
        in_specs=[VMEM] * (CORES + owners),
        out_specs=[ANY, VMEM],
        out_shape=[
            jax.ShapeDtypeStruct((dq[0].shape[0], CORES * dq[0].shape[1]), BF16),
            jax.ShapeDtypeStruct((share, RANK), F32),
        ],
        scratch_shapes=[pltpu.SemaphoreType.DMA((CORES,))],
        name="finish",
        **small(1 << 20),
    )(*dq, *pieces)


def on_device(queries, keys, values, grad_out, docs, block_tenant, low_rank, adapter_b):
    positions, owners = lax.axis_size("ctx"), lax.axis_size("adp")
    chips = positions // CORES
    tokens = queries.shape[0]
    heads_dev = queries.shape[1] // HD
    swap = [(c, c ^ 1) for c in range(positions)]
    up = lambda s: [(c, (c + CORES * s) % positions) for c in range(positions)]
    along = lambda s: [(a, (a + s) % owners) for a in range(owners)]

    message = pack(block_tenant, keys, values, docs, heads_dev)
    shifts = [2, *range(3, chips), 1]
    arrive = {s: lax.ppermute(message, "ctx", up(s)) for s in (2, 1, *range(3, chips))}
    own = [arrive[s] for s in shifts]
    mine_other = lax.ppermute(message, "ctx", swap)
    b_out = columns(adapter_b, mine_other, owners)

    def apart(s):
        return [
            (c * owners + a, c * owners + (a + (s if c % CORES == 0 else -s)) % owners)
            for c in range(positions)
            for a in range(owners)
        ]

    b_in = [lax.ppermute(b_out[s], ("ctx", "adp"), apart(s)) for s in range(1, owners // 2 + 1)]
    heads = (queries, grad_out, message)
    state = attend((0,), *heads, [message], [mine_other])
    own = [*own[1:], own[0]]
    own, state, b_in = lax.optimization_barrier((own, state, b_in))
    other = [lax.ppermute(m, "ctx", swap) for m in own]
    b_swapped = [lax.ppermute(x, "ctx", swap) for x in b_in[:-1]]
    b_cols = [b_out[0], *b_in, *reversed(b_swapped)]
    own, other = [[each[-2], each[-1], *each[:-2]] for each in (own, other)]
    last = functools.partial(attend, tuple(range(1, chips)), *heads, own, other, state)
    dq_other, partner = last((0, low_rank))
    other_part = lax.ppermute(partner, "ctx", swap)
    dq_mine, mine, ranks = last((1, low_rank, dq_other, b_cols))
    pieces = by_tenant(mine, other_part, message, mine_other, ranks, owners)
    pieces = [pieces[0]] + [
        lax.ppermute(pieces[s], "adp", along(s)) for s in range(1, owners)
    ]
    grad_queries, grad_low_rank = finish([dq_other, dq_mine], pieces, tokens // owners)
    pieces = by_columns_owner(pieces)
    pieces = [pieces[0]] + [lax.ppermute(pieces[s], "ctx", up(s)) for s in range(1, chips)]
    grad_adapter = sum(piece.astype(F32) for piece in pieces)[None]
    return grad_queries, grad_low_rank, grad_adapter


def solution(mesh):
    placed = (
        P("ctx", "adp"),
        P("ctx", None),
        P("ctx", None),
        P("ctx", "adp"),
        P("ctx"),
        P("ctx"),
        P("ctx", None),
        P("adp", None, None),
    )
    return jax.shard_map(
        on_device,
        mesh=mesh,
        in_specs=placed,
        out_specs=(P("ctx", "adp"), P(("ctx", "adp"), None), P("adp", None, "ctx")),
        check_vma=False,
    )
```
